256 devices in a mesh: group: 8 (over z), member: 32 (over x, y, core).
Axes of the slice: x: 4, y: 4, z: 8, core: 2. Of those that a mesh axis runs over, the one named last changes fastest.
Arguments:
- hot_table: float32 [768, 1024], replicated, may hold values from -2.4 to 2.4
- hot_state: float32 [768], replicated, may hold values from 0.1 to 10
- cold_table: float32 [16384, 1024], P('member'), may hold values from -2.4 to 2.4
- cold_state: float32 [16384], P('member'), may hold values from 0.1 to 10
- relation_table: float32 [128, 1024], replicated, may hold values from -2.4 to 2.4
- relation_state: float32 [128], replicated, may hold values from 0.1 to 10
- cold_requests: int32 [256, 1024], P(('group', 'member')), may hold values from 0 to 512, as said below
- head_slots: int32 [262144], P(('group', 'member')), may hold values from 0 to 1791, as said below
- relation_index: int32 [262144], P(('group', 'member')), may hold values from 0 to 127
- tail_slots: int32 [262144], P(('group', 'member')), may hold values from 0 to 1791, as said below
- negative_slots: int32 [256, 512], P(('group', 'member')), may hold values from 0 to 1791, as said below
Outputs:
- new_hot_table: float32 [768, 1024], replicated
- new_hot_state: float32 [768], replicated
- new_cold_table: float32 [16384, 1024], P('member')
- new_cold_state: float32 [16384], P('member')
- new_relation_table: float32 [128, 1024], replicated
- new_relation_state: float32 [128], replicated
- mean_loss: float32 [], replicated
The draws below stay inside these ranges and needn't reach their ends.
Inputs may be any that keep to these rules, and one draw needn't show every extreme that they name: `cold_requests`: entries o * 32 onward of a device's row name distinct rows of owner o's block; live entries come first and the rest hold 512; on every device some owner's 32 slots are all live, and one owner's slots are all live on every device. `head_slots`: an entry below 768 is a hot row; else entry - 768 = o * 32 + k is a live slot k of owner o in the list of the device that holds the triple. `tail_slots`: as head_slots. `negative_slots`: as head_slots, for the device that holds the block.
All inputs are finite; a program needn't handle non-finite values.
Results may differ from the reference program's by a relative error of at most 0.0055.
Values may be sent and summed in bfloat16 or wider, within the bound.
No kernel may reach another device: no remote copies, remote signals or barrier semaphores. Data moves between devices by JAX's collectives and lax.ppermute only.
A program may use at most 128 MiB of HBM per device.

```python
import math
import jax
import jax.numpy as jnp
import numpy as np
from jax import lax

DIM = 512
NEG = 512
REL = 128
HOT = 768
COLD_DEV = 512
CAP = 32
STRETCHES_DEV = 1
DEVS = 256
ROWS_DEV = 1024
BATCH = 262144
STRETCHES = 256
COLD_ROWS = 16384
N_MEMBER = 32


def live_counts(key):
    base_key = jax.random.fold_in(key, 101)
    heavy_key, chosen_key, spread_key = jax.random.split(base_key, 3)
    heavy = jax.random.randint(heavy_key, (), 0, N_MEMBER)
    chosen = jax.random.randint(chosen_key, (DEVS, 1), 0, N_MEMBER)
    spread = jax.random.randint(spread_key, (DEVS, N_MEMBER), CAP // 4, CAP // 2 + 1)
    columns = jnp.arange(N_MEMBER)[None, :]
    filled = (columns == heavy) | (columns == chosen)
    return jnp.where(filled, CAP, spread).astype(jnp.int32)


def slot_picks(key, salt, shape, per_device):
    counts = live_counts(key)
    base_key = jax.random.fold_in(key, salt)
    kind_key, hot_key, owner_key, pick_key = jax.random.split(base_key, 4)
    device = jnp.arange(shape[0]) // per_device
    device = device.reshape((shape[0],) + (1,) * (len(shape) - 1)) + jnp.zeros(shape, jnp.int32)
    owner = jax.random.randint(owner_key, shape, 0, N_MEMBER)
    limit = counts[device, owner]
    pick = jax.random.randint(pick_key, shape, 0, 2 ** 20) % limit
    cold_pick = HOT + owner * CAP + pick
    hot_pick = jax.random.randint(hot_key, shape, 0, HOT)
    kind = jax.random.randint(kind_key, shape, 0, 2)
    return jnp.where(kind == 0, hot_pick, cold_pick).astype(jnp.int32)


def draw_cold_requests(key, part):
    counts = live_counts(key).reshape(-1)
    own_key = jax.random.fold_in(key, 7)
    ranks = jax.random.randint(own_key, (DEVS * N_MEMBER, COLD_DEV), 0, 2 ** 20) * COLD_DEV + jnp.arange(COLD_DEV)[None, :]
    order = jnp.argsort(ranks, axis=-1, stable=True)[:, :CAP]
    live = jnp.arange(CAP)[None, :] < counts[:, None]
    return jnp.where(live, order, COLD_DEV).reshape(DEVS, N_MEMBER * CAP).astype(jnp.int32)


def draw_head_slots(key, part):
    return slot_picks(key, 11, (BATCH,), ROWS_DEV)


def draw_tail_slots(key, part):
    return slot_picks(key, 13, (BATCH,), ROWS_DEV)


def draw_negative_slots(key, part):
    return slot_picks(key, 17, (STRETCHES, NEG), STRETCHES_DEV)


def touch_ends(entries, stream_key, smallest, top_value):
    shape = entries.shape
    index_at = [jax.random.randint(jax.random.fold_in(stream_key, axis), (), 0, shape[axis]) for axis in range(len(shape))]
    entries = entries.at[tuple(index_at)].set(smallest)
    longest = shape.index(max(shape))
    index_at[longest] = (index_at[longest] + 1) % shape[longest]
    return entries.at[tuple(index_at)].set(top_value)


def level_of(key, shape, pieces, smallest, largest):
    factor_of, own = 1.0, jax.random.fold_in(key, 6)
    for axis_at, parts in pieces:
        draws = jnp.exp(jax.random.uniform(jax.random.fold_in(own, axis_at), (parts,), jnp.float32, smallest / len(pieces), largest / len(pieces)))
        factor_of = factor_of * jnp.repeat(draws, shape[axis_at] // parts).reshape([-1 if axis == axis_at else 1 for axis in range(len(shape))])
    return factor_of


def rank_bounds(amount, skew):
    portions = [(1 << 20) // math.isqrt(rank ** skew) + 1 for rank in range(1, amount + 1)]
    scale = 1 + sum(portions) // (1 << 30)
    return np.cumsum(np.array([max(1, weight // scale) for weight in portions]))


def ranked_ids(rng, dims, count, skew):
    listing = rank_bounds(count, skew)
    ticket = jax.random.randint(jax.random.fold_in(rng, 1), dims, 0, int(listing[count - 1]))
    standing = jnp.searchsorted(jnp.asarray(listing, jnp.int32), ticket, side="right")
    return jax.random.permutation(jax.random.fold_in(rng, 2), count)[standing].astype(jnp.int32)


def normal_values(stream_key, dims, deviation, most, cuts=(), held_as=jnp.bfloat16):
    level = level_of(stream_key, dims, cuts, -0.22, 0.18) if cuts else 1.0
    entries = jax.random.normal(stream_key, dims, jnp.float32) * deviation * level
    return jnp.minimum(jnp.maximum(entries, -most), most).astype(held_as)


def setup_inputs(seed: int = 0) -> dict:
    key_list = jax.random.split(jax.random.key(seed), 12)
    hot_table = normal_values(key_list[0], (HOT, 2 * DIM), 0.3, 2.4, (), jnp.float32)
    hot_state = jnp.clip(jnp.exp(jax.random.uniform(key_list[1], (HOT,), jnp.float32, math.log(0.1), math.log(10.0))), 0.1, 10.0)
    cold_table = normal_values(key_list[2], (COLD_ROWS, 2 * DIM), 0.3, 2.4, ((0, 32),), jnp.float32)
    cold_state = jnp.clip(jnp.exp(math.log(10.0) - 4.6051702 * jax.random.uniform(key_list[3], (COLD_ROWS,), jnp.float32) ** level_of(key_list[3], (COLD_ROWS,), ((0, 32),), -0.2, 0.2)), 0.1, 10.0)
    relation_table = normal_values(key_list[4], (REL, 2 * DIM), 0.3, 2.4, (), jnp.float32)
    relation_state = jnp.clip(jnp.exp(jax.random.uniform(key_list[5], (REL,), jnp.float32, math.log(0.1), math.log(10.0))), 0.1, 10.0)
    cold_requests = draw_cold_requests(jax.random.fold_in(key_list[11], 71), 0)
    head_slots = draw_head_slots(jax.random.fold_in(key_list[11], 71), 0)
    relation_index = touch_ends(ranked_ids(key_list[8], (BATCH,), REL, 2), jax.random.fold_in(key_list[8], 3), 0, REL - 1).astype(jnp.int32)
    tail_slots = draw_tail_slots(jax.random.fold_in(key_list[11], 71), 0)
    negative_slots = draw_negative_slots(jax.random.fold_in(key_list[11], 71), 0)
    return {"hot_table": hot_table, "hot_state": hot_state, "cold_table": cold_table, "cold_state": cold_state, "relation_table": relation_table, "relation_state": relation_state, "cold_requests": cold_requests, "head_slots": head_slots, "relation_index": relation_index, "tail_slots": tail_slots, "negative_slots": negative_slots}


learn_rate = 0.1

def complex_query(head_rows, relation_rows):
    half_width = head_rows.shape[-1] // 2
    head_real, head_imag = (head_rows[:, :half_width], head_rows[:, half_width:])
    relation_real, relation_imag = (relation_rows[:, :half_width], relation_rows[:, half_width:])
    return jnp.concatenate([head_real * relation_real - head_imag * relation_imag, head_real * relation_imag + head_imag * relation_real], -1)

def query_grads(query_grad, head_rows, relation_rows):
    half_width = head_rows.shape[-1] // 2
    head_real, head_imag = (head_rows[:, :half_width], head_rows[:, half_width:])
    relation_real, relation_imag = (relation_rows[:, :half_width], relation_rows[:, half_width:])
    grad_real, grad_imag = (query_grad[:, :half_width], query_grad[:, half_width:])
    head_grad = jnp.concatenate([grad_real * relation_real + grad_imag * relation_imag, grad_imag * relation_real - grad_real * relation_imag], -1)
    relation_grad = jnp.concatenate([grad_real * head_real + grad_imag * head_imag, grad_imag * head_real - grad_real * head_imag], -1)
    return (head_grad, relation_grad)

def device_terms(entity_rows, relation_half, head_slots, relation_index, tail_slots, negative_slots):
    stretches, neg_count = negative_slots.shape
    row_width = entity_rows.shape[1]
    head_rows = jnp.take(entity_rows, head_slots, axis=0).astype(jnp.float32)
    tail_rows = jnp.take(entity_rows, tail_slots, axis=0).astype(jnp.float32)
    relation_rows = jnp.take(relation_half, relation_index, axis=0).astype(jnp.float32)
    negatives = jnp.take(entity_rows, negative_slots, axis=0).astype(jnp.float32)
    queries = complex_query(head_rows, relation_rows)
    positive = lax.optimization_barrier(jnp.sum(queries * tail_rows, -1))
    blocks = queries.astype(jnp.bfloat16).astype(jnp.float32).reshape(stretches, -1, row_width)
    scores = jnp.einsum('cid,cjd->cij', blocks, negatives)
    loss_sum = jnp.sum(jax.nn.softplus(-positive)) + jnp.sum(jax.nn.softplus(scores)) / neg_count
    pos_grad = jax.nn.sigmoid(positive) - 1.0
    score_grad = (jax.nn.sigmoid(scores) / neg_count).astype(jnp.bfloat16).astype(jnp.float32)
    query_grad = pos_grad[:, None] * tail_rows + jnp.einsum('cij,cjd->cid', score_grad, negatives).reshape(-1, row_width)
    tail_grad = pos_grad[:, None] * queries
    negative_grad = jnp.einsum('cij,cid->cjd', score_grad, blocks).reshape(-1, row_width)
    head_grad, relation_grad = query_grads(query_grad, head_rows, relation_rows)
    all_slots = jnp.concatenate([head_slots, tail_slots, negative_slots.reshape(-1)])
    entity_grad = jax.ops.segment_sum(jnp.concatenate([head_grad, tail_grad, negative_grad]), all_slots, num_segments=entity_rows.shape[0])
    relation_total = jax.ops.segment_sum(relation_grad, relation_index, num_segments=relation_half.shape[0])
    return (loss_sum, entity_grad, relation_total)

def adagrad(emb_table, acc_state, row_grad):
    new_state = acc_state + lax.optimization_barrier(jnp.mean(row_grad * row_grad, -1))
    return (emb_table - learn_rate * row_grad / jnp.sqrt(new_state)[:, None], new_state)

def reference(hot_table, hot_state, cold_table, cold_state, relation_table, relation_state, cold_requests, head_slots, relation_index, tail_slots, negative_slots):
    row_width = hot_table.shape[1]
    cold_count = cold_table.shape[0]
    hot_half = hot_table.astype(jnp.bfloat16)
    cold_half = cold_table.astype(jnp.bfloat16)
    relation_half = relation_table.astype(jnp.bfloat16)
    owners = jnp.arange(N_MEMBER * CAP, dtype=jnp.int32) // CAP

    def one_device(carried, device):
        hot_grad, cold_grad, relation_grad, loss_sum = carried
        wanted = cold_requests[device]
        global_rows = jnp.where(wanted < COLD_DEV, owners * COLD_DEV + wanted, cold_count).astype(jnp.int32)
        fetched = jnp.take(cold_half, global_rows, axis=0, mode='fill', fill_value=0)
        entity_rows = jnp.concatenate([hot_half, fetched])
        row_start = (device * ROWS_DEV).astype(jnp.int32)
        block_start = (device * STRETCHES_DEV).astype(jnp.int32)
        part_loss, entity_grad, relation_part = device_terms(entity_rows, relation_half, lax.dynamic_slice_in_dim(head_slots, row_start, ROWS_DEV), lax.dynamic_slice_in_dim(relation_index, row_start, ROWS_DEV), lax.dynamic_slice_in_dim(tail_slots, row_start, ROWS_DEV), lax.dynamic_slice_in_dim(negative_slots, block_start, STRETCHES_DEV))
        cold_grad = cold_grad + jax.ops.segment_sum(entity_grad[HOT:], global_rows, num_segments=cold_count)
        return ((hot_grad + entity_grad[:HOT], cold_grad, relation_grad + relation_part, loss_sum + part_loss), None)
    start_carry = (jnp.zeros((HOT, row_width), jnp.float32), jnp.zeros((cold_count, row_width), jnp.float32), jnp.zeros((REL, row_width), jnp.float32), jnp.zeros((), jnp.float32))
    totals, _ = lax.scan(one_device, start_carry, jnp.arange(DEVS, dtype=jnp.int32))
    hot_grad, cold_grad, relation_grad, loss_sum = totals
    new_hot_table, new_hot_state = adagrad(hot_table, hot_state, hot_grad)
    new_cold_table, new_cold_state = adagrad(cold_table, cold_state, cold_grad)
    new_relation_table, new_relation_state = adagrad(relation_table, relation_state, relation_grad)
    mean_loss = (loss_sum / BATCH).astype(jnp.float32)
    return (new_hot_table, new_hot_state, new_cold_table, new_cold_state, new_relation_table, new_relation_state, mean_loss)
```

```python
import jax
import jax.numpy as jnp
from jax import lax
from jax.experimental import pallas as pl
from jax.experimental.pallas import tpu as pltpu
from jax.sharding import PartitionSpec as P

learn_rate = 0.1
f32, bf16 = jnp.float32, jnp.bfloat16
TILE = 256
VMEM = pl.BlockSpec(memory_space=pltpu.VMEM)


def dot(lhs, rhs, contract=((1,), (0,))):
    return lax.dot_general(lhs, rhs, (contract, ((), ())), preferred_element_type=f32)


def pick_rows(column, count):
    ids = lax.broadcasted_iota(jnp.int32, (column.shape[0], count), 1)
    return jnp.where(column == ids, 1.0, 0.0).astype(bf16)


def spread_rows(row, first, count):
    ids = lax.broadcasted_iota(jnp.int32, (count, row.shape[1]), 0) + first
    return jnp.where(row == ids, 1.0, 0.0).astype(bf16)


def tiles(total, size=TILE):
    return lambda body: pl.loop(0, total // size)(lambda i: body(pl.ds(pl.multiple_of(i * size, size), size), i))


def serve_kernel(column_ref, table_ref, out_ref, half_ref):
    half_ref[...] = table_ref[...].astype(bf16)

    @tiles(out_ref.shape[0])
    def _(rows, _i):
        hits = pick_rows(column_ref[rows, :], half_ref.shape[0])
        out_ref[rows, :] = dot(hits, half_ref[...]).astype(bf16)


def block_kernel(
    hot_ref, cold_ref, relation_ref, columns_ref, negative_column_ref, slots_ref,
    slot_grad_ref, grads_ref, relation_grads_ref, loss_ref,
    entity, relation_half, heads, tails, relations, negatives, queries, score_grads, pos_grads, query_grads,
):
    hot, half = hot_ref.shape[0], hot_ref.shape[1] // 2
    batch, neg = columns_ref.shape[0], negative_column_ref.shape[0]
    every = entity.shape[0]
    entity[:hot, :] = hot_ref[...].astype(bf16)
    entity[hot:, :] = cold_ref[...]
    relation_half[...] = relation_ref[...].astype(bf16)

    @tiles(neg)
    def _(rows, _i):
        negatives[rows, :] = dot(pick_rows(negative_column_ref[rows, :], every), entity[...]).astype(bf16)

    @tiles(batch)
    def _(rows, _i):
        heads[rows, :] = dot(pick_rows(columns_ref[rows, 0:1], every), entity[...]).astype(bf16)
        tails[rows, :] = dot(pick_rows(columns_ref[rows, 1:2], every), entity[...]).astype(bf16)
        relations[rows, :] = dot(
            pick_rows(columns_ref[rows, 2:3], relation_half.shape[0]), relation_half[...]
        ).astype(bf16)

    def parts(ref, rows):
        both = ref[rows, :].astype(f32)
        return both[:, :half], both[:, half:]

    def query_parts(rows):
        head_real, head_imag = parts(heads, rows)
        relation_real, relation_imag = parts(relations, rows)
        return (
            head_real * relation_real - head_imag * relation_imag,
            head_real * relation_imag + head_imag * relation_real,
        )

    loss_ref[...] = jnp.zeros_like(loss_ref)

    @tiles(batch, 16)
    def _(rows, _i):
        query_real, query_imag = query_parts(rows)
        tail_real, tail_imag = parts(tails, rows)
        positive = jnp.sum(query_real * tail_real + query_imag * tail_imag, -1, keepdims=True)
        queries[rows, :half] = query_real.astype(bf16)
        queries[rows, half:] = query_imag.astype(bf16)
        pos_grads[rows, :] = positive

    positive = pos_grads[...]
    shrunk = jnp.exp(-jnp.abs(positive))
    loss = jnp.sum(jnp.maximum(-positive, 0.0) + jnp.log1p(shrunk))
    pos_grads[...] = jnp.where(positive >= 0, 1.0, shrunk) / (1.0 + shrunk) - 1.0
    loss_ref[...] += loss

    @tiles(batch, 128)
    def _(rows, _i):
        scores = dot(queries[rows, :], negatives[...], ((1,), (1,)))
        shrunk = jnp.exp(-jnp.abs(scores))
        loss = jnp.sum(jnp.maximum(scores, 0.0) + jnp.log1p(shrunk))
        sigmoid = jnp.where(scores >= 0, 1.0, shrunk) / (1.0 + shrunk)
        score_grads[rows, :] = (sigmoid / neg).astype(bf16)
        loss_ref[...] += loss / neg

    @tiles(batch)
    def _(rows, _i):
        query_grads[rows, :] = dot(score_grads[rows, :], negatives[...])

    @tiles(neg)
    def _(rows, i):
        grads_ref[pl.ds(pl.multiple_of(2 * batch + i * TILE, TILE), TILE), :] = dot(
            score_grads[:, pl.ds(pl.multiple_of(i * TILE, TILE), TILE)], queries[...], ((0,), (0,))
        ).astype(bf16)

    @tiles(batch, 16)
    def _(rows, i):
        head_real, head_imag = parts(heads, rows)
        relation_real, relation_imag = parts(relations, rows)
        tail_real, tail_imag = parts(tails, rows)
        pos = pos_grads[rows, :]
        grad_real = query_grads[rows, :half] + pos * tail_real
        grad_imag = query_grads[rows, half:] + pos * tail_imag
        grads_ref[rows, :half] = (grad_real * relation_real + grad_imag * relation_imag).astype(bf16)
        grads_ref[rows, half:] = (grad_imag * relation_real - grad_real * relation_imag).astype(bf16)
        relation_grads_ref[rows, :half] = (grad_real * head_real + grad_imag * head_imag).astype(bf16)
        relation_grads_ref[rows, half:] = (grad_imag * head_real - grad_real * head_imag).astype(bf16)
        later = pl.ds(pl.multiple_of(batch + i * 16, 16), 16)
        grads_ref[later, :half] = (pos * (head_real * relation_real - head_imag * relation_imag)).astype(bf16)
        grads_ref[later, half:] = (pos * (head_real * relation_imag + head_imag * relation_real)).astype(bf16)

    @tiles(every - hot)
    def _(rows, i):
        hits = spread_rows(slots_ref[...], hot + i * TILE, TILE)
        slot_grad_ref[rows, :] = dot(hits, grads_ref[...]).astype(bf16)


def shared_kernel(grads_ref, relation_grads_ref, places_ref, relation_places_ref, loss_ref, out_ref):
    high = loss_ref[...].astype(bf16).astype(f32)
    mid = (loss_ref[...] - high).astype(bf16).astype(f32)
    low = loss_ref[...] - high - mid
    lane = lax.broadcasted_iota(jnp.int32, (1, out_ref.shape[1]), 1)
    pieces = jnp.where(
        lane == 0, high[:1, :1], jnp.where(lane == 1, mid[:1, :1], jnp.where(lane == 2, low[:1, :1], 0.0))
    )

    @tiles(out_ref.shape[0])
    def _(rows, i):
        total = dot(spread_rows(places_ref[...], i * TILE, TILE), grads_ref[...])
        total += dot(spread_rows(relation_places_ref[...], i * TILE, TILE), relation_grads_ref[...])
        place = lax.broadcasted_iota(jnp.int32, (TILE, 1), 0)
        out_ref[rows, :] = jnp.where(place % 32 == 28, pieces, total).astype(bf16)


def owner_kernel(row_ref, arrived_ref, out_ref):
    @tiles(out_ref.shape[0])
    def _(rows, i):
        hits = spread_rows(row_ref[...], i * TILE, TILE)
        out_ref[rows, :] = dot(hits, arrived_ref[...]).astype(bf16)


def params(mib):
    return pltpu.CompilerParams(vmem_limit_bytes=mib * 2**20)


def exchange(array, axis):
    return lax.all_to_all(array, axis, split_axis=0, concat_axis=0, tiled=True)


def adagrad(emb_table, acc_state, row_grad):
    new_state = acc_state + jnp.mean(row_grad * row_grad, -1)
    return (emb_table - learn_rate * row_grad / jnp.sqrt(new_state)[:, None], new_state)


def per_device(
    hot_table, hot_state, cold_table, cold_state, relation_table, relation_state,
    cold_requests, head_slots, relation_index, tail_slots, negative_slots,
):
    members, groups = lax.axis_size("member"), lax.axis_size("group")
    width = hot_table.shape[1]
    hot, owned, relation_count = hot_table.shape[0], cold_table.shape[0], relation_table.shape[0]
    batch, neg = head_slots.shape[0], negative_slots.shape[1]
    asked = cold_requests.shape[1]
    hot_part, relation_part = hot // members, relation_count // members
    shape = jax.ShapeDtypeStruct

    columns = jnp.stack([head_slots, tail_slots, relation_index, relation_index]).T
    slots = jnp.concatenate([head_slots, tail_slots, negative_slots.reshape(-1)])
    places = jnp.where(slots < hot, slots // hot_part * 32 + slots % hot_part, -1).reshape(1, -1)
    slots = slots.reshape(1, -1)
    relation_places = (relation_index // relation_part * 32 + hot_part + relation_index % relation_part).reshape(1, -1)

    received = exchange(cold_requests.reshape(members, -1), "member")
    served = pl.pallas_call(
        serve_kernel, out_shape=shape((asked, width), bf16), in_specs=[VMEM] * 2, out_specs=VMEM,
        scratch_shapes=[pltpu.VMEM((owned, width), bf16)], compiler_params=params(16), name="serve",
    )(received.reshape(-1, 1), cold_table)
    returned = exchange(served.reshape(members, -1, width), "member").reshape(-1, width)

    every = hot + asked
    slot_grads, grads, relation_grads, loss = pl.pallas_call(
        block_kernel,
        out_shape=[
            shape((asked, width), bf16), shape((2 * batch + neg, width), bf16), shape((batch, width), bf16),
            shape((8, 128), f32),
        ],
        in_specs=[VMEM] * 6, out_specs=[VMEM] * 4,
        scratch_shapes=[
            pltpu.VMEM((every, width), bf16), pltpu.VMEM((relation_count, width), bf16),
            pltpu.VMEM((batch, width), bf16), pltpu.VMEM((batch, width), bf16), pltpu.VMEM((batch, width), bf16),
            pltpu.VMEM((neg, width), bf16), pltpu.VMEM((batch, width), bf16), pltpu.VMEM((batch, neg), bf16),
            pltpu.VMEM((batch, 1), f32), pltpu.VMEM((batch, width), f32),
        ],
        compiler_params=params(52), name="block",
    )(hot_table, returned, relation_table, columns, negative_slots.reshape(-1, 1), slots)

    arrived = exchange(slot_grads.reshape(members, -1, width), "member").reshape(-1, width)
    shared = pl.pallas_call(
        shared_kernel, out_shape=shape((32 * members, width), bf16), in_specs=[VMEM] * 5, out_specs=VMEM,
        compiler_params=params(32), name="shared",
    )(grads, relation_grads, places, relation_places, loss)

    owner_grad = pl.pallas_call(
        owner_kernel, out_shape=shape((owned, width), bf16), in_specs=[VMEM] * 2, out_specs=VMEM,
        compiler_params=params(16), name="owner",
    )(received.reshape(1, -1), arrived)
    cold_pieces = exchange(owner_grad.reshape(groups, -1, width), "group")
    cold_piece = jnp.sum(cold_pieces.astype(f32), 0).astype(bf16)
    cold_total = exchange(jnp.broadcast_to(cold_piece[None], (groups,) + cold_piece.shape), "group")
    cold_total = cold_total.reshape(owned, width).astype(f32)

    shared = exchange(shared.reshape(members, -1, width), "member")
    shared = jnp.sum(shared.astype(f32), 0)
    loss = jnp.sum(shared[28])
    high = lax.reduce_precision(loss, 8, 7)
    mid = lax.reduce_precision(loss - high, 8, 7)
    lane = jnp.arange(width)
    pieces = jnp.where(lane == 0, high, jnp.where(lane == 1, mid, jnp.where(lane == 2, loss - high - mid, 0.0)))
    shared = jnp.where(jnp.arange(32)[:, None] == 28, pieces[None], shared).astype(bf16)
    shared = exchange(jnp.broadcast_to(shared[None], (groups,) + shared.shape), "group")
    shared = jnp.sum(shared.astype(f32), 0)
    mean_loss = jnp.sum(shared[28]) / (batch * groups * members)
    shared = shared.astype(bf16)
    shared = exchange(jnp.broadcast_to(shared[None], (members,) + shared.shape), "member").astype(f32)
    hot_total = shared[:, :hot_part].reshape(hot, width)
    relation_total = shared[:, hot_part : hot_part + relation_part].reshape(relation_count, width)

    new_cold_table, new_cold_state = adagrad(cold_table, cold_state, cold_total)
    new_hot_table, new_hot_state = adagrad(hot_table, hot_state, hot_total)
    new_relation_table, new_relation_state = adagrad(relation_table, relation_state, relation_total)
    return (
        new_hot_table, new_hot_state, new_cold_table, new_cold_state,
        new_relation_table, new_relation_state, mean_loss,
    )


def solution(mesh):
    placed = (
        P(), P(), P("member", None), P("member"), P(), P(), P(("group", "member"), None),
        P(("group", "member")), P(("group", "member")), P(("group", "member")), P(("group", "member"), None),
    )
    return jax.shard_map(
        per_device, mesh=mesh, in_specs=placed,
        out_specs=(P(), P(), P("member", None), P("member"), P(), P(), P()), check_vma=False,
    )
```

```python
import functools

import jax
import jax.numpy as jnp
from jax import lax
from jax.experimental import pallas as pl
from jax.experimental.pallas import tpu as pltpu
from jax.sharding import PartitionSpec as P

learn_rate = 0.1
f32, bf16 = jnp.float32, jnp.bfloat16
TILE = 512
STRIP = 16
BUNDLE = 32
LANES = 128
VMEM = pl.BlockSpec(memory_space=pltpu.VMEM)
HBM = pl.BlockSpec(memory_space=pltpu.HBM)
shape = jax.ShapeDtypeStruct


def dot(lhs, rhs, contract=((1,), (0,))):
    return lax.dot_general(lhs, rhs, (contract, ((), ())), preferred_element_type=f32)


def pick_rows(column, first, count):
    ids = lax.broadcasted_iota(jnp.int32, (column.shape[0], count), 1) + first
    return jnp.where(column == ids, 1.0, 0.0).astype(bf16)


def spread_rows(row, ids):
    return jnp.where(row == ids, 1.0, 0.0).astype(bf16)


def row_ids(first, count, width):
    return lax.broadcasted_iota(jnp.int32, (count, width), 0) + first


def at(i, size):
    return pl.ds(pl.multiple_of(i * size, size), size)


def diagonal(count):
    ids = [lax.broadcasted_iota(jnp.int32, (count, count), k) for k in (0, 1)]
    return ids[0] == ids[1]


def to_column(row):
    return jnp.sum(jnp.where(diagonal(row.shape[1]), row, 0.0), 1, keepdims=True)


def to_row(column):
    return jnp.sum(jnp.where(diagonal(column.shape[0]), column, 0.0), 0, keepdims=True)


def serve_kernel(received_ref, half_ref, out_ref, hits, rows_out, sems):
    members, slots = received_ref.shape
    owned = half_ref.shape[0]
    ids = lax.broadcasted_iota(jnp.int32, (slots, owned), 1).astype(f32)
    received = received_ref[...].astype(f32)
    copies = []
    for first in range(0, members * slots, TILE):
        for member in range(first // slots, (first + TILE) // slots):
            column = to_column(received[member : member + 1, :])
            hits[member * slots : (member + 1) * slots, :] = jnp.where(column == ids, 1.0, 0.0).astype(bf16)
        rows = pl.ds(first, TILE)
        rows_out[rows, :] = dot(hits[rows, :], half_ref[...]).astype(bf16)
        copies.append(pltpu.make_async_copy(rows_out.at[rows], out_ref.at[rows], sems.at[first // TILE]))
        copies[-1].start()
    for copy in copies:
        copy.wait()


def early_kernel(hot_ref, relation_ref, columns_ref, negative_column_ref, heads_ref, tails_ref, negatives_ref, relations_ref):
    hot, kinds = hot_ref.shape[0], relation_ref.shape[0]

    @pl.loop(0, negatives_ref.shape[0] // TILE)
    def _(i):
        rows = at(i, TILE)
        negatives_ref[rows, :] = dot(pick_rows(negative_column_ref[rows, :], 0, hot), hot_ref[...]).astype(bf16)

    @pl.loop(0, heads_ref.shape[0] // TILE)
    def _(i):
        rows = at(i, TILE)
        heads_ref[rows, :] = dot(pick_rows(columns_ref[rows, 0:1], 0, hot), hot_ref[...]).astype(bf16)
        tails_ref[rows, :] = dot(pick_rows(columns_ref[rows, 1:2], 0, hot), hot_ref[...]).astype(bf16)
        relations_ref[rows, :] = dot(pick_rows(columns_ref[rows, 2:3], 0, kinds), relation_ref[...]).astype(bf16)


def block_kernel(
    cold_hbm, heads_hbm, tails_hbm, negatives_hbm, relations_hbm, columns_hbm, negative_column_hbm, slots_ref,
    slot_grad_hbm, grads_hbm, relation_grads_hbm, loss_ref,
    cold_ref, heads, tails, negatives, relations, columns_ref, negative_column_ref,
    grads_ref, relation_grads_ref, slot_grad_ref, queries, score_grads, pos_grads, query_grads, sems_in, sems_out,
):
    batch, width = heads.shape
    neg, asked, half = negatives.shape[0], cold_ref.shape[0], width // 2
    hot = 768
    pairs = (
        (cold_hbm, cold_ref), (negative_column_hbm, negative_column_ref), (negatives_hbm, negatives),
        (columns_hbm, columns_ref), (heads_hbm, heads), (tails_hbm, tails), (relations_hbm, relations),
    )
    copies = [pltpu.make_async_copy(source, target, sems_in.at[k]) for k, (source, target) in enumerate(pairs)]
    for copy in copies:
        copy.start()
    for copy in copies[:3]:
        copy.wait()

    def add_cold(target, column_ref, lane):
        @pl.loop(0, target.shape[0] // TILE)
        def _(i):
            rows = at(i, TILE)
            found = dot(pick_rows(column_ref[rows, lane : lane + 1], hot, asked), cold_ref[...])
            target[rows, :] = (found + target[rows, :].astype(f32)).astype(bf16)

    add_cold(negatives, negative_column_ref, 0)
    for copy in copies[3:]:
        copy.wait()
    add_cold(heads, columns_ref, 0)
    add_cold(tails, columns_ref, 1)

    def parts(ref, rows):
        both = ref[rows, :].astype(f32)
        return both[:, :half], both[:, half:]

    @pl.loop(0, batch // STRIP, unroll=4)
    def _(i):
        rows = at(i, STRIP)
        head_real, head_imag = parts(heads, rows)
        relation_real, relation_imag = parts(relations, rows)
        query_real = head_real * relation_real - head_imag * relation_imag
        query_imag = head_real * relation_imag + head_imag * relation_real
        tail_real, tail_imag = parts(tails, rows)
        queries[rows, :half] = query_real.astype(bf16)
        queries[rows, half:] = query_imag.astype(bf16)
        pos_grads[rows, :] = jnp.sum(query_real * tail_real + query_imag * tail_imag, -1, keepdims=True)

    positive = pos_grads[...]
    shrunk = jnp.exp(-jnp.abs(positive))
    loss_ref[...] = jnp.full_like(loss_ref, jnp.sum(jnp.maximum(-positive, 0.0) + jnp.log1p(shrunk)))
    pos_grads[...] = jnp.where(positive >= 0, 1.0, shrunk) / (1.0 + shrunk) - 1.0

    @pl.loop(0, batch // 128, unroll=2)
    def _(i):
        rows = at(i, 128)
        scores = dot(queries[rows, :], negatives[...], ((1,), (1,)))
        shrunk = jnp.exp(-jnp.abs(scores))
        loss = jnp.sum(jnp.maximum(scores, 0.0) + jnp.log1p(shrunk))
        sigmoid = jnp.where(scores >= 0, 1.0, shrunk) / (1.0 + shrunk)
        score_grads[rows, :] = (sigmoid / neg).astype(bf16)
        loss_ref[...] += loss / neg

    @pl.loop(0, batch // TILE)
    def _(i):
        rows = at(i, TILE)
        query_grads[rows, :] = dot(score_grads[rows, :], negatives[...])

    grads_ref[2 * batch :, :] = dot(score_grads[...], queries[...], ((0,), (0,))).astype(bf16)

    @pl.loop(0, batch // STRIP, unroll=4)
    def _(i):
        rows = at(i, STRIP)
        head_real, head_imag = parts(heads, rows)
        relation_real, relation_imag = parts(relations, rows)
        tail_real, tail_imag = parts(tails, rows)
        pos = pos_grads[rows, :]
        grad_real = query_grads[rows, :half] + pos * tail_real
        grad_imag = query_grads[rows, half:] + pos * tail_imag
        grads_ref[rows, :half] = (grad_real * relation_real + grad_imag * relation_imag).astype(bf16)
        grads_ref[rows, half:] = (grad_imag * relation_real - grad_real * relation_imag).astype(bf16)
        relation_grads_ref[rows, :half] = (grad_real * head_real + grad_imag * head_imag).astype(bf16)
        relation_grads_ref[rows, half:] = (grad_imag * head_real - grad_real * head_imag).astype(bf16)
        later = pl.ds(pl.multiple_of(batch + i * STRIP, STRIP), STRIP)
        grads_ref[later, :half] = (pos * (head_real * relation_real - head_imag * relation_imag)).astype(bf16)
        grads_ref[later, half:] = (pos * (head_real * relation_imag + head_imag * relation_real)).astype(bf16)

    copies = [
        pltpu.make_async_copy(grads_ref, grads_hbm, sems_out.at[0]),
        pltpu.make_async_copy(relation_grads_ref, relation_grads_hbm, sems_out.at[1]),
    ]
    for copy in copies:
        copy.start()
    for i in range(asked // TILE):
        rows = pl.ds(i * TILE, TILE)
        hits = spread_rows(slots_ref[...], row_ids(hot + i * TILE, TILE, 1))
        slot_grad_ref[rows, :] = dot(hits, grads_ref[...]).astype(bf16)
        copies.append(pltpu.make_async_copy(slot_grad_ref.at[rows], slot_grad_hbm.at[rows], sems_out.at[2 + i]))
        copies[-1].start()
    for copy in copies:
        copy.wait()


def loss_pieces(loss, width):
    high = loss.astype(bf16).astype(f32)
    mid = (loss - high).astype(bf16).astype(f32)
    lane = lax.broadcasted_iota(jnp.int32, (1, width), 1)
    return jnp.where(lane == 0, high, jnp.where(lane == 1, mid, jnp.where(lane == 2, loss - high - mid, 0.0)))


def shared_kernel(loss_at, grads_ref, relation_grads_ref, places_ref, relation_places_ref, loss_ref, mine_ref, other_ref):
    count, width = mine_ref.shape
    pieces = loss_pieces(loss_ref[:1, :1], width)
    place = row_ids(0, count, 1)
    for i, out_ref in enumerate((mine_ref, other_ref)):
        ids = row_ids(i * count, count, 1)
        total = dot(spread_rows(places_ref[...], ids), grads_ref[...])
        total += dot(spread_rows(relation_places_ref[...], ids), relation_grads_ref[...])
        out_ref[...] = jnp.where(place % BUNDLE == loss_at, pieces, total).astype(out_ref.dtype)


def total_of(parts):
    return sum((part.astype(f32) for part in parts[1:]), parts[0].astype(f32))


def owner_kernel(row_ref, arrived_ref, mine_ref, other_ref, owner_ref, shared_ref):
    shared_ref[...] = (mine_ref[...] + other_ref[...].astype(f32)).astype(bf16)
    hits = spread_rows(row_ref[...], row_ids(0, owner_ref.shape[0], 1))
    owner_ref[...] = dot(hits, arrived_ref[...]).astype(bf16)


def member_sum_kernel(loss_at, parts_ref, out_ref):
    total = total_of([parts_ref[k] for k in range(parts_ref.shape[0])])
    loss = jnp.sum(total[loss_at : loss_at + 1, :], -1, keepdims=True)
    total = jnp.where(row_ids(0, BUNDLE, 1) == loss_at, loss_pieces(loss, total.shape[1]), total).astype(bf16)
    for k in range(out_ref.shape[0]):
        out_ref[k] = total


def group_sum_kernel(loss_at, batch_total, parts_ref, _after, shared_ref, loss_ref):
    total = total_of([parts_ref[k] for k in range(parts_ref.shape[0])])
    loss = jnp.sum(total[loss_at : loss_at + 1, :], -1, keepdims=True)
    loss_ref[...] = jnp.broadcast_to(loss / batch_total, loss_ref.shape)
    total = total.astype(bf16)
    for k in range(shared_ref.shape[0]):
        shared_ref[k] = total


def stepped(table, state_row, grad):
    new_state = to_column(state_row) + jnp.mean(grad * grad, -1, keepdims=True)
    return table - learn_rate * grad / jnp.sqrt(new_state), to_row(new_state)


def cold_step_kernel(grad_ref, table_ref, state_ref, new_table, new_state):
    at_row = pl.ds(pl.program_id(0), 1)
    new_table[...], new_state[at_row, :] = stepped(table_ref[...], state_ref[at_row, :], grad_ref[...].astype(f32))


def shared_step_kernel(
    shared_ref, hot_ref, hot_state_ref, relation_ref, relation_state_ref,
    new_hot, new_hot_state, new_relation, new_relation_state, grads,
):
    step = pl.program_id(0)

    @pl.when(step == 0)
    def _():
        members = shared_ref.shape[0] // BUNDLE
        hot_part, relation_part = grads.shape[0] // members, relation_ref.shape[0] // members
        relation_grad = []
        for member in range(members):
            bundle = shared_ref[member * BUNDLE : (member + 1) * BUNDLE, :].astype(f32)
            grads[member * hot_part : (member + 1) * hot_part, :] = bundle[:hot_part, :]
            relation_grad.append(bundle[hot_part : hot_part + relation_part, :])
        new_relation[...], new_relation_state[...] = stepped(
            relation_ref[...], relation_state_ref[...], jnp.concatenate(relation_grad)
        )

    at_row = pl.ds(step, 1)
    new_hot[...], new_hot_state[at_row, :] = stepped(hot_ref[...], hot_state_ref[at_row, :], grads[at(step, LANES), :])


def call(kernel, name, out_shape, args, mib, flops=0, in_spaces=None, out_spaces=None, scratch=()):
    several = isinstance(out_shape, list)
    out_spaces = out_spaces or [VMEM] * (len(out_shape) if several else 1)
    return pl.pallas_call(
        kernel,
        out_shape=out_shape,
        in_specs=in_spaces or [VMEM] * len(args),
        out_specs=out_spaces if several else out_spaces[0],
        scratch_shapes=scratch,
        compiler_params=pltpu.CompilerParams(vmem_limit_bytes=mib * 2**20),
        cost_estimate=pl.CostEstimate(flops=flops, bytes_accessed=0, transcendentals=0),
        name=name,
    )(*args)


def exchange(array, axis, within=None):
    return lax.all_to_all(array, axis, split_axis=0, concat_axis=0, tiled=True, axis_index_groups=within)


def per_device(
    hot_table, hot_state, cold_table, cold_state, relation_table, relation_state,
    cold_requests, head_slots, relation_index, tail_slots, negative_slots,
):
    members, groups = lax.axis_size("member"), lax.axis_size("group")
    chips = members // 2
    width = hot_table.shape[1]
    hot, owned, relation_count = hot_table.shape[0], cold_table.shape[0], relation_table.shape[0]
    batch, neg = head_slots.shape[0], negative_slots.shape[1]
    asked = cold_requests.shape[1]
    hot_part, relation_part = hot // members, relation_count // members
    core = lax.axis_index("member") % 2
    same_core = [list(range(k, members, 2)) for k in (0, 1)]
    swap = [(m, m ^ 1) for m in range(members)]

    def place_of(owner, within):
        return ((owner % 2 ^ core) * chips + owner // 2) * BUNDLE + within

    received = exchange(cold_requests.reshape(members, -1), "member")
    cold_half = cold_table.astype(bf16)
    served = call(
        serve_kernel, "serve", shape((asked, width), bf16), (received, cold_half), 61, 2 * asked * owned * width,
        out_spaces=[HBM],
        scratch=[
            pltpu.VMEM((asked, owned), bf16), pltpu.VMEM((asked, width), bf16),
            pltpu.SemaphoreType.DMA((asked // TILE,)),
        ],
    )
    returned = exchange(served.reshape(members, -1, width), "member").reshape(-1, width)

    columns = jnp.stack([head_slots, tail_slots, relation_index, relation_index]).T
    negative_column = negative_slots.reshape(-1, 1)
    slots = jnp.concatenate([head_slots, tail_slots, negative_slots.reshape(-1)])
    places = jnp.where(slots < hot, place_of(slots // hot_part, slots % hot_part), -1).reshape(1, -1)
    slots = slots.reshape(1, -1)
    relation_places = place_of(relation_index // relation_part, hot_part + relation_index % relation_part)

    rows, batch_rows = 2 * batch + neg, shape((batch, width), bf16)
    hot_heads, hot_tails, hot_negatives, relations = call(
        early_kernel, "early", [batch_rows, batch_rows, shape((neg, width), bf16), batch_rows],
        (hot_table.astype(bf16), relation_table.astype(bf16), columns, negative_column), 24,
        2 * rows * hot * width,
    )
    slot_grads, grads, relation_grads, loss = call(
        block_kernel, "block",
        [shape((asked, width), bf16), shape((rows, width), bf16), batch_rows, shape((8, 128), f32)],
        (returned, hot_heads, hot_tails, hot_negatives, relations, columns, negative_column, slots), 61,
        4 * rows * asked * width + 6 * batch * neg * width,
        in_spaces=[HBM] * 7 + [VMEM], out_spaces=[HBM] * 3 + [VMEM],
        scratch=[
            pltpu.VMEM((asked, width), bf16), pltpu.VMEM((batch, width), bf16), pltpu.VMEM((batch, width), bf16),
            pltpu.VMEM((neg, width), bf16), pltpu.VMEM((batch, width), bf16), pltpu.VMEM(columns.shape, jnp.int32),
            pltpu.VMEM((neg, 1), jnp.int32), pltpu.VMEM((rows, width), bf16), pltpu.VMEM((batch, width), bf16),
            pltpu.VMEM((asked, width), bf16), pltpu.VMEM((batch, width), bf16), pltpu.VMEM((batch, neg), bf16),
            pltpu.VMEM((batch, 1), f32), pltpu.VMEM((batch, width), f32), pltpu.SemaphoreType.DMA((7,)),
            pltpu.SemaphoreType.DMA((2 + asked // TILE,)),
        ],
    )
    arrived = exchange(slot_grads.reshape(members, -1, width), "member").reshape(-1, width)

    half, loss_at = chips * BUNDLE, hot_part + relation_part
    mine, other = call(
        functools.partial(shared_kernel, loss_at), "shared",
        [shape((half, width), f32), shape((half, width), bf16)],
        (grads, relation_grads, places, relation_places.reshape(1, -1), loss), 32, 4 * half * (rows + batch) * width,
    )
    other = lax.ppermute(other, "member", swap)
    owner_grad, shared = call(
        owner_kernel, "owner", [shape((owned, width), bf16), shape((half, width), bf16)],
        (received.reshape(1, -1), arrived, mine, other), 24, 2 * asked * owned * width,
    )
    cold_piece = lax.psum_scatter(owner_grad, "group", scatter_dimension=0, tiled=True)
    shared = exchange(shared.reshape(chips, -1, width), "member", same_core)
    shared = call(
        functools.partial(member_sum_kernel, loss_at), "member_sum", shape((groups, BUNDLE, width), bf16), (shared,), 8
    )
    shared, mean_loss = call(
        functools.partial(group_sum_kernel, loss_at, batch * groups * members), "group_sum",
        [shape((members, BUNDLE, width), bf16), shape((8, 128), f32)], (exchange(shared, "group"), cold_piece), 8,
        in_spaces=[VMEM, HBM],
    )
    cold_total = lax.all_gather(cold_piece, "group", axis=0, tiled=True)
    shared = exchange(shared, "member").reshape(-1, width)
    full = lambda *dims: pl.BlockSpec(dims, lambda i: (0,) * len(dims))
    step_rows = pl.BlockSpec((LANES, width), lambda i: (i, 0))
    hot_rows, relation_rows, cold_rows = hot // LANES, relation_count // LANES, owned // LANES
    new_hot_table, new_hot_state, new_relation_table, new_relation_state = pl.pallas_call(
        shared_step_kernel,
        grid=(hot_rows,),
        out_shape=[
            shape((hot, width), f32), shape((hot_rows, LANES), f32),
            shape((relation_count, width), f32), shape((relation_rows, LANES), f32),
        ],
        in_specs=[
            full(*shared.shape), step_rows, full(hot_rows, LANES), full(relation_count, width), full(relation_rows, LANES),
        ],
        out_specs=[step_rows, full(hot_rows, LANES), full(relation_count, width), full(relation_rows, LANES)],
        scratch_shapes=[pltpu.VMEM((hot, width), f32)],
        compiler_params=pltpu.CompilerParams(vmem_limit_bytes=20 * 2**20),
        name="shared_step",
    )(shared, hot_table, hot_state.reshape(-1, LANES), relation_table, relation_state.reshape(-1, LANES))
    new_cold_table, new_cold_state = pl.pallas_call(
        cold_step_kernel,
        grid=(cold_rows,),
        out_shape=[shape((owned, width), f32), shape((cold_rows, LANES), f32)],
        in_specs=[step_rows, step_rows, full(cold_rows, LANES)],
        out_specs=[step_rows, full(cold_rows, LANES)],
        compiler_params=pltpu.CompilerParams(vmem_limit_bytes=12 * 2**20),
        name="cold_step",
    )(cold_total, cold_table, cold_state.reshape(-1, LANES))
    return (
        new_hot_table, new_hot_state.reshape(-1), new_cold_table, new_cold_state.reshape(-1),
        new_relation_table, new_relation_state.reshape(-1), mean_loss[0, 0],
    )


def solution(mesh):
    placed = (
        P(), P(), P("member", None), P("member"), P(), P(), P(("group", "member"), None),
        P(("group", "member")), P(("group", "member")), P(("group", "member")), P(("group", "member"), None),
    )
    return jax.shard_map(
        per_device, mesh=mesh, in_specs=placed,
        out_specs=(P(), P(), P("member", None), P("member"), P(), P(), P()), check_vma=False,
    )
```

```python
import functools

import jax
import jax.numpy as jnp
from jax import lax
from jax.experimental import pallas as pl
from jax.experimental.pallas import tpu as pltpu
from jax.sharding import PartitionSpec as P

learn_rate = 0.1
f32, bf16 = jnp.float32, jnp.bfloat16
TILE = 512
STRIP = 16
BUNDLE = 32
LANES = 128
VMEM = pl.BlockSpec(memory_space=pltpu.VMEM)
HBM = pl.BlockSpec(memory_space=pltpu.HBM)
SMEM = pl.BlockSpec(memory_space=pltpu.SMEM)
shape = jax.ShapeDtypeStruct


def dot(lhs, rhs, contract=((1,), (0,))):
    return lax.dot_general(lhs, rhs, (contract, ((), ())), preferred_element_type=f32)


def pick_rows(column, first, count):
    ids = lax.broadcasted_iota(jnp.int32, (column.shape[0], count), 1) + first
    return jnp.where(column == ids, 1.0, 0.0).astype(bf16)


def spread_rows(row, ids):
    return jnp.where(row == ids, 1.0, 0.0).astype(bf16)


def row_ids(first, count, width):
    return lax.broadcasted_iota(jnp.int32, (count, width), 0) + first


def at(i, size):
    return pl.ds(pl.multiple_of(i * size, size), size)


def diagonal(count):
    ids = [lax.broadcasted_iota(jnp.int32, (count, count), k) for k in (0, 1)]
    return ids[0] == ids[1]


def to_column(row):
    return jnp.sum(jnp.where(diagonal(row.shape[1]), row, 0.0), 1, keepdims=True)


def to_row(column):
    return jnp.sum(jnp.where(diagonal(column.shape[0]), column, 0.0), 0, keepdims=True)


def requests_kernel(wanted_ref, out_ref):
    members, _, slots = out_ref.shape
    for member in range(members):
        out_ref[member] = wanted_ref[:, member * slots : (member + 1) * slots]


def serve_kernel(received_ref, half_ref, out_ref, hits, rows_out, sems):
    members, _, slots = received_ref.shape
    owned = half_ref.shape[0]
    ids = lax.broadcasted_iota(jnp.int32, (slots, owned), 1).astype(f32)
    copies = []
    for first in range(0, members * slots, TILE):
        for member in range(first // slots, (first + TILE) // slots):
            column = to_column(received_ref[member].astype(f32))
            hits[member * slots : (member + 1) * slots, :] = jnp.where(column == ids, 1.0, 0.0).astype(bf16)
        rows = pl.ds(first, TILE)
        rows_out[rows, :] = dot(hits[rows, :], half_ref[...]).astype(bf16)
        copies.append(pltpu.make_async_copy(rows_out.at[rows], out_ref.at[rows], sems.at[first // TILE]))
        copies[-1].start()
    for copy in copies:
        copy.wait()


def early_kernel(hot_ref, relation_ref, columns_ref, negative_column_ref, heads_ref, tails_ref, negatives_ref, relations_ref):
    hot, kinds = hot_ref.shape[0], relation_ref.shape[0]

    @pl.loop(0, negatives_ref.shape[0] // TILE)
    def _(i):
        rows = at(i, TILE)
        negatives_ref[rows, :] = dot(pick_rows(negative_column_ref[rows, :], 0, hot), hot_ref[...]).astype(bf16)

    @pl.loop(0, heads_ref.shape[0] // TILE)
    def _(i):
        rows = at(i, TILE)
        heads_ref[rows, :] = dot(pick_rows(columns_ref[rows, 0:1], 0, hot), hot_ref[...]).astype(bf16)
        tails_ref[rows, :] = dot(pick_rows(columns_ref[rows, 1:2], 0, hot), hot_ref[...]).astype(bf16)
        relations_ref[rows, :] = dot(pick_rows(columns_ref[rows, 2:3], 0, kinds), relation_ref[...]).astype(bf16)


def block_kernel(
    cold_hbm, heads_hbm, tails_hbm, negatives_hbm, relations_hbm, columns_hbm, negative_column_hbm, slots_ref,
    slot_grad_hbm, grads_hbm, relation_grads_hbm, loss_ref,
    cold_ref, heads, tails, negatives, relations, columns_ref, negative_column_ref,
    grads_ref, relation_grads_ref, slot_grad_ref, queries, score_grads, pos_grads, query_grads, sems_in, sems_out,
):
    batch, width = heads.shape
    neg, asked, half = negatives.shape[0], cold_ref.shape[0], width // 2
    hot = 768
    pairs = (
        (cold_hbm, cold_ref), (negative_column_hbm, negative_column_ref), (negatives_hbm, negatives),
        (columns_hbm, columns_ref), (heads_hbm, heads), (tails_hbm, tails), (relations_hbm, relations),
    )
    copies = [pltpu.make_async_copy(source, target, sems_in.at[k]) for k, (source, target) in enumerate(pairs)]
    for copy in copies:
        copy.start()
    for copy in copies[:3]:
        copy.wait()

    def add_cold(target, column_ref, lane):
        @pl.loop(0, target.shape[0] // TILE)
        def _(i):
            rows = at(i, TILE)
            found = dot(pick_rows(column_ref[rows, lane : lane + 1], hot, asked), cold_ref[...])
            target[rows, :] = (found + target[rows, :].astype(f32)).astype(bf16)

    add_cold(negatives, negative_column_ref, 0)
    for copy in copies[3:]:
        copy.wait()
    add_cold(heads, columns_ref, 0)
    add_cold(tails, columns_ref, 1)

    def parts(ref, rows):
        both = ref[rows, :].astype(f32)
        return both[:, :half], both[:, half:]

    @pl.loop(0, batch // STRIP, unroll=4)
    def _(i):
        rows = at(i, STRIP)
        head_real, head_imag = parts(heads, rows)
        relation_real, relation_imag = parts(relations, rows)
        query_real = head_real * relation_real - head_imag * relation_imag
        query_imag = head_real * relation_imag + head_imag * relation_real
        tail_real, tail_imag = parts(tails, rows)
        queries[rows, :half] = query_real.astype(bf16)
        queries[rows, half:] = query_imag.astype(bf16)
        pos_grads[rows, :] = jnp.sum(query_real * tail_real + query_imag * tail_imag, -1, keepdims=True)

    positive = pos_grads[...]
    shrunk = jnp.exp(-jnp.abs(positive))
    loss_ref[...] = jnp.full_like(loss_ref, jnp.sum(jnp.maximum(-positive, 0.0) + jnp.log1p(shrunk)))
    pos_grads[...] = jnp.where(positive >= 0, 1.0, shrunk) / (1.0 + shrunk) - 1.0

    @pl.loop(0, batch // 128, unroll=2)
    def _(i):
        rows = at(i, 128)
        scores = dot(queries[rows, :], negatives[...], ((1,), (1,)))
        shrunk = jnp.exp(-jnp.abs(scores))
        loss = jnp.sum(jnp.maximum(scores, 0.0) + jnp.log1p(shrunk))
        sigmoid = jnp.where(scores >= 0, 1.0, shrunk) / (1.0 + shrunk)
        score_grads[rows, :] = (sigmoid / neg).astype(bf16)
        loss_ref[...] += loss / neg

    @pl.loop(0, batch // TILE)
    def _(i):
        rows = at(i, TILE)
        query_grads[rows, :] = dot(score_grads[rows, :], negatives[...])

    grads_ref[2 * batch :, :] = dot(score_grads[...], queries[...], ((0,), (0,))).astype(bf16)

    @pl.loop(0, batch // STRIP, unroll=4)
    def _(i):
        rows = at(i, STRIP)
        head_real, head_imag = parts(heads, rows)
        relation_real, relation_imag = parts(relations, rows)
        tail_real, tail_imag = parts(tails, rows)
        pos = pos_grads[rows, :]
        grad_real = query_grads[rows, :half] + pos * tail_real
        grad_imag = query_grads[rows, half:] + pos * tail_imag
        grads_ref[rows, :half] = (grad_real * relation_real + grad_imag * relation_imag).astype(bf16)
        grads_ref[rows, half:] = (grad_imag * relation_real - grad_real * relation_imag).astype(bf16)
        relation_grads_ref[rows, :half] = (grad_real * head_real + grad_imag * head_imag).astype(bf16)
        relation_grads_ref[rows, half:] = (grad_imag * head_real - grad_real * head_imag).astype(bf16)
        later = pl.ds(pl.multiple_of(batch + i * STRIP, STRIP), STRIP)
        grads_ref[later, :half] = (pos * (head_real * relation_real - head_imag * relation_imag)).astype(bf16)
        grads_ref[later, half:] = (pos * (head_real * relation_imag + head_imag * relation_real)).astype(bf16)

    copies = [
        pltpu.make_async_copy(grads_ref, grads_hbm, sems_out.at[0]),
        pltpu.make_async_copy(relation_grads_ref, relation_grads_hbm, sems_out.at[1]),
    ]
    for copy in copies:
        copy.start()
    for i in range(asked // TILE):
        rows = pl.ds(i * TILE, TILE)
        hits = spread_rows(slots_ref[...], row_ids(hot + i * TILE, TILE, 1))
        slot_grad_ref[rows, :] = dot(hits, grads_ref[...]).astype(bf16)
        copies.append(pltpu.make_async_copy(slot_grad_ref.at[rows], slot_grad_hbm.at[rows], sems_out.at[2 + i]))
        copies[-1].start()
    for copy in copies:
        copy.wait()


def loss_pieces(loss, width):
    high = loss.astype(bf16).astype(f32)
    mid = (loss - high).astype(bf16).astype(f32)
    lane = lax.broadcasted_iota(jnp.int32, (1, width), 1)
    return jnp.where(lane == 0, high, jnp.where(lane == 1, mid, jnp.where(lane == 2, loss - high - mid, 0.0)))


def shared_kernel(loss_at, grads_ref, relation_grads_ref, places_ref, relation_places_ref, loss_ref, mine_ref, other_ref):
    count, width = mine_ref.shape
    pieces = loss_pieces(loss_ref[:1, :1], width)
    place = row_ids(0, count, 1)
    for i, out_ref in enumerate((mine_ref, other_ref)):
        ids = row_ids(i * count, count, 1)
        total = dot(spread_rows(places_ref[...], ids), grads_ref[...])
        total += dot(spread_rows(relation_places_ref[...], ids), relation_grads_ref[...])
        out_ref[...] = jnp.where(place % BUNDLE == loss_at, pieces, total).astype(out_ref.dtype)


def total_of(parts):
    return sum((part.astype(f32) for part in parts[1:]), parts[0].astype(f32))


def chip_sum_kernel(mine_ref, other_ref, shared_ref):
    shared_ref[...] = (mine_ref[...] + other_ref[...].astype(f32)).astype(bf16)


def owner_kernel(group_ref, row_ref, arrived_ref, _shared, _same, *out_refs):
    groups, piece = len(out_refs), out_refs[0].shape[0]
    total = row_ids(0, groups * piece, 1)
    ids = (total // piece + group_ref[0]) % groups * piece + total % piece
    found = dot(spread_rows(row_ref[...], ids), arrived_ref[...])
    for k, out_ref in enumerate(out_refs):
        out_ref[...] = found[k * piece : (k + 1) * piece, :].astype(bf16)


def cold_sum_kernel(*refs):
    refs[-1][...] = total_of([ref[...] for ref in refs[:-1]]).astype(bf16)


def member_sum_kernel(loss_at, parts_ref, _after, out_ref):
    total = total_of([parts_ref[k] for k in range(parts_ref.shape[0])])
    loss = jnp.sum(total[loss_at : loss_at + 1, :], -1, keepdims=True)
    total = jnp.where(row_ids(0, BUNDLE, 1) == loss_at, loss_pieces(loss, total.shape[1]), total).astype(bf16)
    for k in range(out_ref.shape[0]):
        out_ref[k] = total


def group_sum_kernel(loss_at, batch_total, parts_ref, *refs):
    shared_ref, loss_ref = refs[-2:]
    total = total_of([parts_ref[k] for k in range(parts_ref.shape[0])])
    loss = jnp.sum(total[loss_at : loss_at + 1, :], -1, keepdims=True)
    loss_ref[...] = jnp.broadcast_to(loss / batch_total, loss_ref.shape)
    total = total.astype(bf16)
    for k in range(shared_ref.shape[0]):
        shared_ref[k] = total


def stepped(table, state_row, grad):
    new_state = to_column(state_row) + jnp.mean(grad * grad, -1, keepdims=True)
    return table - grad * (learn_rate / jnp.sqrt(new_state)), to_row(new_state)


def stream_steps(jobs, sems_in, sems_out):
    blocks = [(job, k) for job in jobs for k in range(job[1].shape[0] // LANES)]
    part = lambda k: pl.ds(k * LANES, LANES)
    loads = [
        pltpu.make_async_copy(job[0].at[part(k)], job[1].at[part(k)], sems_in.at[n]) for n, (job, k) in enumerate(blocks)
    ]
    stores = [
        pltpu.make_async_copy(job[5].at[part(k)], job[4].at[part(k)], sems_out.at[n]) for n, (job, k) in enumerate(blocks)
    ]
    for load in loads:
        load.start()

    def run():
        for load, store, (job, k) in zip(loads, stores, blocks):
            _, table, state, grad, _, result, new_state = job
            load.wait()
            result[part(k), :], new_state[k : k + 1, :] = stepped(
                table[part(k), :], state[k : k + 1, :], grad[part(k), :].astype(f32)
            )
            store.start()
        for store in stores:
            store.wait()

    return run


def cold_step_kernel(group_ref, table_hbm, state_ref, *refs):
    pieces, (new_table, new_state, table, result, grads, sems_in, sems_out) = refs[:-7], refs[-7:]
    run = stream_steps([(table_hbm, table, state_ref, grads, new_table, result, new_state)], sems_in, sems_out)
    groups, piece = len(pieces), pieces[0].shape[0]
    for k, piece_ref in enumerate(pieces):
        grads[at(lax.rem(group_ref[0] + groups - k, groups), piece), :] = piece_ref[...]
    run()


def shared_step_kernel(
    core_ref, mine_ref, other_ref, hot_hbm, hot_state, relation_hbm, relation_state, new_hot, new_hot_state, new_relation, new_relation_state,
    hot_table, hot_result, hot_grads, relation_table, relation_result, relation_grads, sems_in, sems_out,
):
    run = stream_steps(
        [
            (hot_hbm, hot_table, hot_state, hot_grads, new_hot, hot_result, new_hot_state),
            (relation_hbm, relation_table, relation_state, relation_grads, new_relation, relation_result, new_relation_state),
        ],
        sems_in, sems_out,
    )
    members = 2 * mine_ref.shape[0] // BUNDLE
    hot_part, relation_part = hot_grads.shape[0] // members, relation_grads.shape[0] // members
    first = core_ref[0] == 0
    for member in range(0, members, 2):
        rows = slice(member // 2 * BUNDLE, (member // 2 + 1) * BUNDLE)
        mine, other = mine_ref[rows, :].astype(f32), other_ref[rows, :].astype(f32)
        pair = (jnp.where(first, mine, other), jnp.where(first, other, mine))
        for k, grad in enumerate(pair):
            hot_grads[(member + k) * hot_part : (member + k + 1) * hot_part, :] = grad[:hot_part, :]
        relation_grads[member * relation_part : (member + 2) * relation_part, :] = jnp.concatenate(
            [grad[hot_part : hot_part + relation_part, :] for grad in pair]
        )
    run()


def call(kernel, name, out_shape, args, mib, flops=0, in_spaces=None, out_spaces=None, scratch=(), aliases=None):
    several = isinstance(out_shape, list)
    out_spaces = out_spaces or [VMEM] * (len(out_shape) if several else 1)
    return pl.pallas_call(
        kernel,
        out_shape=out_shape,
        in_specs=in_spaces or [VMEM] * len(args),
        out_specs=out_spaces if several else out_spaces[0],
        scratch_shapes=scratch,
        input_output_aliases=aliases or {},
        compiler_params=pltpu.CompilerParams(vmem_limit_bytes=mib * 2**20),
        cost_estimate=pl.CostEstimate(flops=flops, bytes_accessed=0, transcendentals=0),
        name=name,
    )(*args)


def exchange(array, axis, within=None):
    return lax.all_to_all(array, axis, split_axis=0, concat_axis=0, tiled=True, axis_index_groups=within)


def per_device(
    hot_table, hot_state, cold_table, cold_state, relation_table, relation_state,
    cold_requests, head_slots, relation_index, tail_slots, negative_slots,
):
    members, groups = lax.axis_size("member"), lax.axis_size("group")
    chips = members // 2
    width = hot_table.shape[1]
    hot, owned, relation_count = hot_table.shape[0], cold_table.shape[0], relation_table.shape[0]
    batch, neg = head_slots.shape[0], negative_slots.shape[1]
    asked = cold_requests.shape[1]
    hot_part, relation_part = hot // members, relation_count // members
    core = lax.axis_index("member") % 2
    group_at, core_at = lax.axis_index("group").reshape(1), core.reshape(1)
    same_core = [list(range(k, members, 2)) for k in (0, 1)]
    swap = [(m, m ^ 1) for m in range(members)]

    def place_of(owner, within):
        return ((owner % 2 ^ core) * chips + owner // 2) * BUNDLE + within

    wanted = call(requests_kernel, "requests", shape((members, 1, asked // members), jnp.int32), (cold_requests,), 61)
    received = exchange(wanted, "member")
    cold_half = cold_table.astype(bf16)
    served = call(
        serve_kernel, "serve", shape((asked, width), bf16), (received, cold_half), 61, 2 * asked * owned * width,
        out_spaces=[HBM],
        scratch=[
            pltpu.VMEM((asked, owned), bf16), pltpu.VMEM((asked, width), bf16),
            pltpu.SemaphoreType.DMA((asked // TILE,)),
        ],
    )
    returned = exchange(served.reshape(members, -1, width), "member").reshape(-1, width)

    columns = jnp.stack([head_slots, tail_slots, relation_index, relation_index]).T
    negative_column = negative_slots.reshape(-1, 1)
    slots = jnp.concatenate([head_slots, tail_slots, negative_slots.reshape(-1)])
    places = jnp.where(slots < hot, place_of(slots // hot_part, slots % hot_part), -1).reshape(1, -1)
    slots = slots.reshape(1, -1)
    relation_places = place_of(relation_index // relation_part, hot_part + relation_index % relation_part)

    rows, batch_rows = 2 * batch + neg, shape((batch, width), bf16)
    hot_heads, hot_tails, hot_negatives, relations = call(
        early_kernel, "early", [batch_rows, batch_rows, shape((neg, width), bf16), batch_rows],
        (hot_table.astype(bf16), relation_table.astype(bf16), columns, negative_column), 24,
        2 * rows * hot * width,
    )
    slot_grads, grads, relation_grads, loss = call(
        block_kernel, "block",
        [shape((asked, width), bf16), shape((rows, width), bf16), batch_rows, shape((8, 128), f32)],
        (returned, hot_heads, hot_tails, hot_negatives, relations, columns, negative_column, slots), 61,
        4 * rows * asked * width + 6 * batch * neg * width,
        in_spaces=[HBM] * 7 + [VMEM], out_spaces=[HBM] * 3 + [VMEM],
        scratch=[
            pltpu.VMEM((asked, width), bf16), pltpu.VMEM((batch, width), bf16), pltpu.VMEM((batch, width), bf16),
            pltpu.VMEM((neg, width), bf16), pltpu.VMEM((batch, width), bf16), pltpu.VMEM(columns.shape, jnp.int32),
            pltpu.VMEM((neg, 1), jnp.int32), pltpu.VMEM((rows, width), bf16), pltpu.VMEM((batch, width), bf16),
            pltpu.VMEM((asked, width), bf16), pltpu.VMEM((batch, width), bf16), pltpu.VMEM((batch, neg), bf16),
            pltpu.VMEM((batch, 1), f32), pltpu.VMEM((batch, width), f32), pltpu.SemaphoreType.DMA((7,)),
            pltpu.SemaphoreType.DMA((2 + asked // TILE,)),
        ],
    )
    arrived = exchange(slot_grads.reshape(members, -1, width), "member").reshape(-1, width)

    half, loss_at = chips * BUNDLE, hot_part + relation_part
    mine, other = call(
        functools.partial(shared_kernel, loss_at), "shared",
        [shape((half, width), f32), shape((half, width), bf16)],
        (grads, relation_grads, places, relation_places.reshape(1, -1), loss), 32, 4 * half * (rows + batch) * width,
    )
    other = lax.ppermute(other, "member", swap)
    shared = call(chip_sum_kernel, "chip_sum", shape((half, width), bf16), (mine, other), 8)
    piece = owned // groups
    shared, *pieces = call(
        owner_kernel, "owner", [shape((half, width), bf16)] + [shape((piece, width), bf16)] * groups,
        (group_at, received.reshape(1, -1), arrived, shared), 24, 2 * asked * owned * width,
        in_spaces=[SMEM, VMEM, VMEM, HBM], out_spaces=[HBM] + [VMEM] * groups, aliases={3: 0},
    )
    ways = [(k, [(g, (g + k) % groups) for g in range(groups)]) for k in range(1, groups)]
    pieces = [pieces[0]] + [lax.ppermute(pieces[k], "group", way) for k, way in ways]
    cold_piece = call(cold_sum_kernel, "cold_sum", shape((piece, width), bf16), pieces, 8)

    shared = exchange(shared.reshape(chips, -1, width), "member", same_core)
    shared = call(
        functools.partial(member_sum_kernel, loss_at), "member_sum", shape((groups, BUNDLE, width), bf16),
        (shared, cold_piece), 8, in_spaces=[VMEM, HBM],
    )
    sent = {k: lax.ppermute(cold_piece, "group", way) for k, way in ways}
    near, far = [sent[k] for k in (1, 7, 2, 6)], [sent[k] for k in (3, 5, 4)]
    shared, mean_loss = call(
        functools.partial(group_sum_kernel, loss_at, batch * groups * members), "group_sum",
        [shape((chips, BUNDLE, width), bf16), shape((8, 128), f32)], (exchange(shared, "group"), *near), 8,
        in_spaces=[VMEM] + [HBM] * len(near),
    )
    pieces = [cold_piece] + [sent[k] for k in range(1, groups)]
    mine = exchange(shared, "member", same_core).reshape(-1, width)
    mine = call(
        lambda *refs: None, "after_far", shape(mine.shape, bf16), (mine, *far), 8,
        in_spaces=[HBM] * (1 + len(far)), out_spaces=[HBM], aliases={0: 0},
    )
    other = lax.ppermute(mine, "member", swap)
    state = lambda array: array.reshape(-1, LANES)
    buffers = lambda count: [pltpu.VMEM((count, width), f32), pltpu.VMEM((count, width), f32)]
    sems = lambda count: [pltpu.SemaphoreType.DMA((count // LANES,))] * 2
    new_cold_table, new_cold_state = call(
        cold_step_kernel, "cold_step", [shape((owned, width), f32), shape((owned // LANES, LANES), f32)],
        (group_at, cold_table, state(cold_state), *pieces), 61,
        in_spaces=[SMEM, HBM] + [VMEM] * (groups + 1), out_spaces=[HBM, VMEM],
        scratch=buffers(owned) + [pltpu.VMEM((owned, width), bf16)] + sems(owned),
    )
    new_hot_table, new_hot_state, new_relation_table, new_relation_state = call(
        shared_step_kernel, "shared_step",
        [
            shape((hot, width), f32), shape((hot // LANES, LANES), f32),
            shape((relation_count, width), f32), shape((relation_count // LANES, LANES), f32),
        ],
        (core_at, mine, other, hot_table, state(hot_state), relation_table, state(relation_state)), 61,
        in_spaces=[SMEM, VMEM, VMEM, HBM, VMEM, HBM, VMEM], out_spaces=[HBM, VMEM, HBM, VMEM],
        scratch=buffers(hot) + [pltpu.VMEM((hot, width), f32)] + buffers(relation_count)
        + [pltpu.VMEM((relation_count, width), f32)] + sems(hot + relation_count),
    )
    return (
        new_hot_table, new_hot_state.reshape(-1), new_cold_table, new_cold_state.reshape(-1),
        new_relation_table, new_relation_state.reshape(-1), mean_loss[0, 0],
    )


def solution(mesh):
    placed = (
        P(), P(), P("member", None), P("member"), P(), P(), P(("group", "member"), None),
        P(("group", "member")), P(("group", "member")), P(("group", "member")), P(("group", "member"), None),
    )
    return jax.shard_map(
        per_device, mesh=mesh, in_specs=placed,
        out_specs=(P(), P(), P("member", None), P("member"), P(), P(), P()), check_vma=False,
    )
```

```python
import functools

import jax
import jax.numpy as jnp
from jax import lax
from jax.experimental import pallas as pl
from jax.experimental.pallas import tpu as pltpu
from jax.sharding import PartitionSpec as P

learn_rate = 0.1
f32, bf16 = jnp.float32, jnp.bfloat16
TILE = 512
STEP = 256
STRIP = 16
BUNDLE = 32
LANES = 128
VMEM = pl.BlockSpec(memory_space=pltpu.VMEM)
HBM = pl.BlockSpec(memory_space=pltpu.HBM)
SMEM = pl.BlockSpec(memory_space=pltpu.SMEM)
shape = jax.ShapeDtypeStruct


def dot(lhs, rhs, contract=((1,), (0,))):
    return lax.dot_general(lhs, rhs, (contract, ((), ())), preferred_element_type=f32)


def pick_rows(column, first, count):
    ids = lax.broadcasted_iota(jnp.int32, (column.shape[0], count), 1) + first
    return jnp.where(column == ids, 1.0, 0.0).astype(bf16)


def spread_rows(row, ids):
    return jnp.where(row == ids, 1.0, 0.0).astype(bf16)


def row_ids(first, count, width):
    return lax.broadcasted_iota(jnp.int32, (count, width), 0) + first


def at(i, size):
    return pl.ds(pl.multiple_of(i * size, size), size)


def diagonal(count):
    ids = [lax.broadcasted_iota(jnp.int32, (count, count), k) for k in (0, 1)]
    return ids[0] == ids[1]


def to_column(row):
    return jnp.sum(jnp.where(diagonal(row.shape[1]), row, 0.0), 1, keepdims=True)


def to_row(column):
    return jnp.sum(jnp.where(diagonal(column.shape[0]), column, 0.0), 0, keepdims=True)


def requests_kernel(wanted_ref, out_ref):
    members, _, slots = out_ref.shape
    for member in range(members):
        out_ref[member] = wanted_ref[:, member * slots : (member + 1) * slots]


def serve_kernel(received_ref, half_ref, out_ref, hits, rows_out, sems):
    members, _, slots = received_ref.shape
    owned = half_ref.shape[0]
    ids = lax.broadcasted_iota(jnp.int32, (slots, owned), 1).astype(f32)
    copies = []
    for first in range(0, members * slots, TILE):
        for member in range(first // slots, (first + TILE) // slots):
            column = to_column(received_ref[member].astype(f32))
            hits[member * slots : (member + 1) * slots, :] = jnp.where(column == ids, 1.0, 0.0).astype(bf16)
        rows = pl.ds(first, TILE)
        rows_out[rows, :] = dot(hits[rows, :], half_ref[...]).astype(bf16)
        copies.append(pltpu.make_async_copy(rows_out.at[rows], out_ref.at[rows], sems.at[first // TILE]))
        copies[-1].start()
    for copy in copies:
        copy.wait()


def early_kernel(hot_ref, relation_ref, columns_ref, negative_column_ref, heads_ref, tails_ref, negatives_ref, relations_ref):
    hot, kinds = hot_ref.shape[0], relation_ref.shape[0]

    @pl.loop(0, negatives_ref.shape[0] // TILE)
    def _(i):
        rows = at(i, TILE)
        negatives_ref[rows, :] = dot(pick_rows(negative_column_ref[rows, :], 0, hot), hot_ref[...]).astype(bf16)

    @pl.loop(0, heads_ref.shape[0] // TILE)
    def _(i):
        rows = at(i, TILE)
        heads_ref[rows, :] = dot(pick_rows(columns_ref[rows, 0:1], 0, hot), hot_ref[...]).astype(bf16)
        tails_ref[rows, :] = dot(pick_rows(columns_ref[rows, 1:2], 0, hot), hot_ref[...]).astype(bf16)
        relations_ref[rows, :] = dot(pick_rows(columns_ref[rows, 2:3], 0, kinds), relation_ref[...]).astype(bf16)


def block_kernel(
    cold_hbm, heads_hbm, tails_hbm, negatives_hbm, relations_hbm, columns_hbm, negative_column_hbm, slots_ref,
    slot_grad_hbm, grads_hbm, relation_grads_hbm, loss_ref,
    cold_ref, heads, tails, negatives, relations, columns_ref, negative_column_ref,
    grads_ref, relation_grads_ref, slot_grad_ref, queries, score_grads, pos_grads, query_grads, sems_in, sems_out,
):
    batch, width = heads.shape
    neg, asked, half = negatives.shape[0], cold_ref.shape[0], width // 2
    hot = 768
    pairs = (
        (cold_hbm, cold_ref), (negative_column_hbm, negative_column_ref), (negatives_hbm, negatives),
        (columns_hbm, columns_ref), (heads_hbm, heads), (tails_hbm, tails), (relations_hbm, relations),
    )
    copies = [pltpu.make_async_copy(source, target, sems_in.at[k]) for k, (source, target) in enumerate(pairs)]
    for copy in copies:
        copy.start()
    for copy in copies[:3]:
        copy.wait()

    def add_cold(target, column_ref, lane):
        for i in range(target.shape[0] // STEP):
            rows = pl.ds(i * STEP, STEP)
            found = dot(pick_rows(column_ref[rows, lane : lane + 1], hot, asked), cold_ref[...])
            target[rows, :] = (found + target[rows, :].astype(f32)).astype(bf16)

    add_cold(negatives, negative_column_ref, 0)
    for copy in copies[3:]:
        copy.wait()
    add_cold(heads, columns_ref, 0)
    add_cold(tails, columns_ref, 1)

    def parts(ref, rows):
        both = ref[rows, :].astype(f32)
        return both[:, :half], both[:, half:]

    @pl.loop(0, batch // STRIP, unroll=16)
    def _(i):
        rows = at(i, STRIP)
        head_real, head_imag = parts(heads, rows)
        relation_real, relation_imag = parts(relations, rows)
        query_real = head_real * relation_real - head_imag * relation_imag
        query_imag = head_real * relation_imag + head_imag * relation_real
        tail_real, tail_imag = parts(tails, rows)
        queries[rows, :half] = query_real.astype(bf16)
        queries[rows, half:] = query_imag.astype(bf16)
        pos_grads[rows, :] = jnp.sum(query_real * tail_real + query_imag * tail_imag, -1, keepdims=True)

    positive = pos_grads[...]
    shrunk = jnp.exp(-jnp.abs(positive))
    loss_ref[...] = jnp.full_like(loss_ref, jnp.sum(jnp.maximum(-positive, 0.0) + jnp.log1p(shrunk)))
    pos_grads[...] = jnp.where(positive >= 0, 1.0, shrunk) / (1.0 + shrunk) - 1.0

    for i in range(batch // STEP):
        rows = pl.ds(i * STEP, STEP)
        scores = dot(queries[rows, :], negatives[...], ((1,), (1,)))
        shrunk = jnp.exp(-jnp.abs(scores))
        loss = jnp.sum(jnp.maximum(scores, 0.0) + jnp.log1p(shrunk))
        sigmoid = jnp.where(scores >= 0, 1.0, shrunk) / (1.0 + shrunk)
        score_grads[rows, :] = (sigmoid / neg).astype(bf16)
        loss_ref[...] += loss / neg

    for i in range(batch // STEP):
        rows = pl.ds(i * STEP, STEP)
        query_grads[rows, :] = dot(score_grads[rows, :], negatives[...])

    grads_ref[2 * batch :, :] = dot(score_grads[...], queries[...], ((0,), (0,))).astype(bf16)

    @pl.loop(0, batch // STRIP, unroll=16)
    def _(i):
        rows = at(i, STRIP)
        head_real, head_imag = parts(heads, rows)
        relation_real, relation_imag = parts(relations, rows)
        tail_real, tail_imag = parts(tails, rows)
        pos = pos_grads[rows, :]
        grad_real = query_grads[rows, :half] + pos * tail_real
        grad_imag = query_grads[rows, half:] + pos * tail_imag
        grads_ref[rows, :half] = (grad_real * relation_real + grad_imag * relation_imag).astype(bf16)
        grads_ref[rows, half:] = (grad_imag * relation_real - grad_real * relation_imag).astype(bf16)
        relation_grads_ref[rows, :half] = (grad_real * head_real + grad_imag * head_imag).astype(bf16)
        relation_grads_ref[rows, half:] = (grad_imag * head_real - grad_real * head_imag).astype(bf16)
        later = pl.ds(pl.multiple_of(batch + i * STRIP, STRIP), STRIP)
        grads_ref[later, :half] = (pos * (head_real * relation_real - head_imag * relation_imag)).astype(bf16)
        grads_ref[later, half:] = (pos * (head_real * relation_imag + head_imag * relation_real)).astype(bf16)

    copies = [
        pltpu.make_async_copy(grads_ref, grads_hbm, sems_out.at[0]),
        pltpu.make_async_copy(relation_grads_ref, relation_grads_hbm, sems_out.at[1]),
    ]
    for copy in copies:
        copy.start()
    for i in range(asked // TILE):
        rows = pl.ds(i * TILE, TILE)
        hits = spread_rows(slots_ref[...], row_ids(hot + i * TILE, TILE, 1))
        slot_grad_ref[rows, :] = dot(hits, grads_ref[...]).astype(bf16)
        copies.append(pltpu.make_async_copy(slot_grad_ref.at[rows], slot_grad_hbm.at[rows], sems_out.at[2 + i]))
        copies[-1].start()
    for copy in copies:
        copy.wait()


def loss_pieces(loss, width):
    high = loss.astype(bf16).astype(f32)
    mid = (loss - high).astype(bf16).astype(f32)
    lane = lax.broadcasted_iota(jnp.int32, (1, width), 1)
    return jnp.where(lane == 0, high, jnp.where(lane == 1, mid, jnp.where(lane == 2, loss - high - mid, 0.0)))


def shared_kernel(loss_at, grads_ref, relation_grads_ref, places_ref, relation_places_ref, loss_ref, mine_ref, other_ref):
    count, width = mine_ref.shape
    pieces = loss_pieces(loss_ref[:1, :1], width)
    place = row_ids(0, count, 1)
    for i, out_ref in enumerate((mine_ref, other_ref)):
        ids = row_ids(i * count, count, 1)
        total = dot(spread_rows(places_ref[...], ids), grads_ref[...])
        total += dot(spread_rows(relation_places_ref[...], ids), relation_grads_ref[...])
        out_ref[...] = jnp.where(place % BUNDLE == loss_at, pieces, total).astype(out_ref.dtype)


def total_of(parts):
    return sum((part.astype(f32) for part in parts[1:]), parts[0].astype(f32))


def chip_sum_kernel(mine_ref, other_ref, shared_ref):
    shared_ref[...] = (mine_ref[...] + other_ref[...].astype(f32)).astype(bf16)


def group_rows(group, offsets, groups, piece):
    return jnp.concatenate([row_ids(lax.rem(group + offset, groups) * piece, piece, 1) for offset in offsets])


def owner_kernel(group_ref, row_ref, arrived_ref, _shared, _same, up_ref, down_ref, far_up_ref, far_down_ref, kept_ref):
    piece = far_up_ref.shape[0]
    ids = group_rows(group_ref[0], (1, 5, 7, 3, 2, 6, 0, 4), 8, piece)
    found = dot(spread_rows(row_ref[...], ids), arrived_ref[...])
    first = 0
    for ref in (up_ref, down_ref, far_up_ref, far_down_ref, kept_ref):
        ref[...] = found[first : first + ref.shape[0], :].astype(ref.dtype)
        first += ref.shape[0]


def near_sum_kernel(kept_ref, up_ref, down_ref, far_up_ref, far_down_ref, out_ref):
    piece = far_up_ref.shape[0]
    total = total_of([kept_ref[...], up_ref[...], down_ref[...]])
    out_ref[:piece, :] = total_of([total[:piece, :], far_up_ref[...], far_down_ref[...]]).astype(bf16)
    out_ref[piece:, :] = total[piece:, :].astype(bf16)


def member_sum_kernel(loss_at, parts_ref, _after, out_ref):
    total = total_of([parts_ref[k] for k in range(parts_ref.shape[0])])
    loss = jnp.sum(total[loss_at : loss_at + 1, :], -1, keepdims=True)
    total = jnp.where(row_ids(0, BUNDLE, 1) == loss_at, loss_pieces(loss, total.shape[1]), total).astype(bf16)
    for k in range(out_ref.shape[0]):
        out_ref[k] = total


def group_sum_kernel(loss_at, batch_total, parts_ref, near_ref, across_ref, shared_ref, loss_ref, pair_ref, own_ref):
    piece = own_ref.shape[0]
    own = total_of([near_ref[:piece, :], across_ref[piece:, :]]).astype(bf16)
    own_ref[...] = own
    pair_ref[:piece, :] = own
    pair_ref[piece:, :] = total_of([near_ref[piece:, :], across_ref[:piece, :]]).astype(bf16)
    total = total_of([parts_ref[k] for k in range(parts_ref.shape[0])])
    loss = jnp.sum(total[loss_at : loss_at + 1, :], -1, keepdims=True)
    loss_ref[...] = jnp.broadcast_to(loss / batch_total, loss_ref.shape)
    total = total.astype(bf16)
    for k in range(shared_ref.shape[0]):
        shared_ref[k] = total


def stepped(table, state_row, grad):
    new_state = to_column(state_row) + jnp.mean(grad * grad, -1, keepdims=True)
    return table - grad * (learn_rate / jnp.sqrt(new_state)), to_row(new_state)


def stream_steps(jobs, sems_in, sems_out):
    blocks = [(job, k) for job in jobs for k in range(job[1].shape[0] // LANES)]
    part = lambda k: pl.ds(k * LANES, LANES)
    loads = [
        pltpu.make_async_copy(job[0].at[part(k)], job[1].at[part(k)], sems_in.at[n]) for n, (job, k) in enumerate(blocks)
    ]
    stores = [
        pltpu.make_async_copy(job[5].at[part(k)], job[4].at[part(k)], sems_out.at[n]) for n, (job, k) in enumerate(blocks)
    ]
    for load in loads:
        load.start()

    def run():
        for load, store, (job, k) in zip(loads, stores, blocks):
            _, table, state, grad, _, result, new_state = job
            load.wait()
            result[part(k), :], new_state[k : k + 1, :] = stepped(
                table[part(k), :], state[k : k + 1, :], grad[part(k), :].astype(f32)
            )
            store.start()
        for store in stores:
            store.wait()

    return run


def cold_step_kernel(group_ref, table_hbm, state_ref, *refs):
    pieces, (new_table, new_state, table, result, grads, sems_in, sems_out) = refs[:-7], refs[-7:]
    run = stream_steps([(table_hbm, table, state_ref, grads, new_table, result, new_state)], sems_in, sems_out)
    for piece_ref, offsets in zip(pieces, ((0, 4), (7, 3), (1, 5), (6,), (2,))):
        size = piece_ref.shape[0] // len(offsets)
        for k, offset in enumerate(offsets):
            rows = at(lax.rem(group_ref[0] + offset, grads.shape[0] // size), size)
            grads[rows, :] = piece_ref[k * size : (k + 1) * size, :]
    run()


def shared_step_kernel(
    core_ref, mine_ref, other_ref, hot_hbm, hot_state, relation_hbm, relation_state, new_hot, new_hot_state, new_relation, new_relation_state,
    hot_table, hot_result, hot_grads, relation_table, relation_result, relation_grads, sems_in, sems_out,
):
    run = stream_steps(
        [
            (hot_hbm, hot_table, hot_state, hot_grads, new_hot, hot_result, new_hot_state),
            (relation_hbm, relation_table, relation_state, relation_grads, new_relation, relation_result, new_relation_state),
        ],
        sems_in, sems_out,
    )
    members = 2 * mine_ref.shape[0] // BUNDLE
    hot_part, relation_part = hot_grads.shape[0] // members, relation_grads.shape[0] // members
    first = core_ref[0] == 0
    for member in range(0, members, 2):
        rows = slice(member // 2 * BUNDLE, (member // 2 + 1) * BUNDLE)
        mine, other = mine_ref[rows, :].astype(f32), other_ref[rows, :].astype(f32)
        pair = (jnp.where(first, mine, other), jnp.where(first, other, mine))
        for k, grad in enumerate(pair):
            hot_grads[(member + k) * hot_part : (member + k + 1) * hot_part, :] = grad[:hot_part, :]
        relation_grads[member * relation_part : (member + 2) * relation_part, :] = jnp.concatenate(
            [grad[hot_part : hot_part + relation_part, :] for grad in pair]
        )
    run()


def call(kernel, name, out_shape, args, mib, flops=0, in_spaces=None, out_spaces=None, scratch=(), aliases=None):
    several = isinstance(out_shape, list)
    out_spaces = out_spaces or [VMEM] * (len(out_shape) if several else 1)
    return pl.pallas_call(
        kernel,
        out_shape=out_shape,
        in_specs=in_spaces or [VMEM] * len(args),
        out_specs=out_spaces if several else out_spaces[0],
        scratch_shapes=scratch,
        input_output_aliases=aliases or {},
        compiler_params=pltpu.CompilerParams(vmem_limit_bytes=mib * 2**20),
        cost_estimate=pl.CostEstimate(flops=flops, bytes_accessed=0, transcendentals=0),
        name=name,
    )(*args)


def exchange(array, axis, within=None):
    return lax.all_to_all(array, axis, split_axis=0, concat_axis=0, tiled=True, axis_index_groups=within)


def per_device(
    hot_table, hot_state, cold_table, cold_state, relation_table, relation_state,
    cold_requests, head_slots, relation_index, tail_slots, negative_slots,
):
    members, groups = lax.axis_size("member"), lax.axis_size("group")
    chips = members // 2
    width = hot_table.shape[1]
    hot, owned, relation_count = hot_table.shape[0], cold_table.shape[0], relation_table.shape[0]
    batch, neg = head_slots.shape[0], negative_slots.shape[1]
    asked = cold_requests.shape[1]
    hot_part, relation_part = hot // members, relation_count // members
    core = lax.axis_index("member") % 2
    group_at, core_at = lax.axis_index("group").reshape(1), core.reshape(1)
    same_core = [list(range(k, members, 2)) for k in (0, 1)]
    swap = [(m, m ^ 1) for m in range(members)]

    def place_of(owner, within):
        return ((owner % 2 ^ core) * chips + owner // 2) * BUNDLE + within

    wanted = call(requests_kernel, "requests", shape((members, 1, asked // members), jnp.int32), (cold_requests,), 61)
    received = exchange(wanted, "member")
    cold_half = cold_table.astype(bf16)
    served = call(
        serve_kernel, "serve", shape((asked, width), bf16), (received, cold_half), 61, 2 * asked * owned * width,
        out_spaces=[HBM],
        scratch=[
            pltpu.VMEM((asked, owned), bf16), pltpu.VMEM((asked, width), bf16),
            pltpu.SemaphoreType.DMA((asked // TILE,)),
        ],
    )
    returned = exchange(served.reshape(members, -1, width), "member").reshape(-1, width)

    columns = jnp.stack([head_slots, tail_slots, relation_index, relation_index]).T
    negative_column = negative_slots.reshape(-1, 1)
    slots = jnp.concatenate([head_slots, tail_slots, negative_slots.reshape(-1)])
    places = jnp.where(slots < hot, place_of(slots // hot_part, slots % hot_part), -1).reshape(1, -1)
    slots = slots.reshape(1, -1)
    relation_places = place_of(relation_index // relation_part, hot_part + relation_index % relation_part)

    rows, batch_rows = 2 * batch + neg, shape((batch, width), bf16)
    hot_heads, hot_tails, hot_negatives, relations = call(
        early_kernel, "early", [batch_rows, batch_rows, shape((neg, width), bf16), batch_rows],
        (hot_table.astype(bf16), relation_table.astype(bf16), columns, negative_column), 24,
        2 * rows * hot * width,
    )
    slot_grads, grads, relation_grads, loss = call(
        block_kernel, "block",
        [shape((asked, width), bf16), shape((rows, width), bf16), batch_rows, shape((8, 128), f32)],
        (returned, hot_heads, hot_tails, hot_negatives, relations, columns, negative_column, slots), 61,
        4 * rows * asked * width + 6 * batch * neg * width,
        in_spaces=[HBM] * 7 + [VMEM], out_spaces=[HBM] * 3 + [VMEM],
        scratch=[
            pltpu.VMEM((asked, width), bf16), pltpu.VMEM((batch, width), bf16), pltpu.VMEM((batch, width), bf16),
            pltpu.VMEM((neg, width), bf16), pltpu.VMEM((batch, width), bf16), pltpu.VMEM(columns.shape, jnp.int32),
            pltpu.VMEM((neg, 1), jnp.int32), pltpu.VMEM((rows, width), bf16), pltpu.VMEM((batch, width), bf16),
            pltpu.VMEM((asked, width), bf16), pltpu.VMEM((batch, width), bf16), pltpu.VMEM((batch, neg), bf16),
            pltpu.VMEM((batch, 1), f32), pltpu.VMEM((batch, width), f32), pltpu.SemaphoreType.DMA((7,)),
            pltpu.SemaphoreType.DMA((2 + asked // TILE,)),
        ],
    )
    arrived = exchange(slot_grads.reshape(members, -1, width), "member").reshape(-1, width)

    half, loss_at = chips * BUNDLE, hot_part + relation_part
    mine, other = call(
        functools.partial(shared_kernel, loss_at), "shared",
        [shape((half, width), f32), shape((half, width), bf16)],
        (grads, relation_grads, places, relation_places.reshape(1, -1), loss), 32, 4 * half * (rows + batch) * width,
    )
    other = lax.ppermute(other, "member", swap)
    shared = call(chip_sum_kernel, "chip_sum", shape((half, width), bf16), (mine, other), 8)
    piece = owned // groups
    one, two = shape((piece, width), bf16), shape((2 * piece, width), bf16)
    shared, up, down, far_up, far_down, kept = call(
        owner_kernel, "owner", [shape((half, width), bf16), two, two, one, one, shape((2 * piece, width), f32)],
        (group_at, received.reshape(1, -1), arrived, shared), 24, 2 * asked * owned * width,
        in_spaces=[SMEM, VMEM, VMEM, HBM], out_spaces=[HBM] + [VMEM] * 5, aliases={3: 0},
    )
    hop = lambda array, k: lax.ppermute(array, "group", [(g, (g + k) % groups) for g in range(groups)])
    near = call(near_sum_kernel, "near_sum", two, (kept, hop(up, 1), hop(down, -1), hop(far_up, 2), hop(far_down, -2)), 8)

    shared = exchange(shared.reshape(chips, -1, width), "member", same_core)
    shared = call(
        functools.partial(member_sum_kernel, loss_at), "member_sum", shape((groups, BUNDLE, width), bf16),
        (shared, near), 8, in_spaces=[VMEM, HBM],
    )
    across = hop(near, 4)
    shared, mean_loss, pair, own = call(
        functools.partial(group_sum_kernel, loss_at, batch * groups * members), "group_sum",
        [shape((chips, BUNDLE, width), bf16), shape((8, 128), f32), two, one],
        (exchange(shared, "group"), near, across), 8,
    )
    sent = [hop(pair, 1), hop(pair, -1), hop(own, 2), hop(own, -2)]
    pieces = [pair] + sent
    mine = exchange(shared, "member", same_core).reshape(-1, width)
    mine = call(
        lambda *refs: None, "after_sent", shape(mine.shape, bf16), (mine, *sent), 8,
        in_spaces=[HBM] * (1 + len(sent)), out_spaces=[HBM], aliases={0: 0},
    )
    other = lax.ppermute(mine, "member", swap)
    state = lambda array: array.reshape(-1, LANES)
    buffers = lambda count: [pltpu.VMEM((count, width), f32), pltpu.VMEM((count, width), f32)]
    sems = lambda count: [pltpu.SemaphoreType.DMA((count // LANES,))] * 2
    new_cold_table, new_cold_state = call(
        cold_step_kernel, "cold_step", [shape((owned, width), f32), shape((owned // LANES, LANES), f32)],
        (group_at, cold_table, state(cold_state), *pieces), 61,
        in_spaces=[SMEM, HBM] + [VMEM] * (1 + len(pieces)), out_spaces=[HBM, VMEM],
        scratch=buffers(owned) + [pltpu.VMEM((owned, width), bf16)] + sems(owned),
    )
    new_hot_table, new_hot_state, new_relation_table, new_relation_state = call(
        shared_step_kernel, "shared_step",
        [
            shape((hot, width), f32), shape((hot // LANES, LANES), f32),
            shape((relation_count, width), f32), shape((relation_count // LANES, LANES), f32),
        ],
        (core_at, mine, other, hot_table, state(hot_state), relation_table, state(relation_state)), 61,
        in_spaces=[SMEM, VMEM, VMEM, HBM, VMEM, HBM, VMEM], out_spaces=[HBM, VMEM, HBM, VMEM],
        scratch=buffers(hot) + [pltpu.VMEM((hot, width), f32)] + buffers(relation_count)
        + [pltpu.VMEM((relation_count, width), f32)] + sems(hot + relation_count),
    )
    return (
        new_hot_table, new_hot_state.reshape(-1), new_cold_table, new_cold_state.reshape(-1),
        new_relation_table, new_relation_state.reshape(-1), mean_loss[0, 0],
    )


def solution(mesh):
    placed = (
        P(), P(), P("member", None), P("member"), P(), P(), P(("group", "member"), None),
        P(("group", "member")), P(("group", "member")), P(("group", "member")), P(("group", "member"), None),
    )
    return jax.shard_map(
        per_device, mesh=mesh, in_specs=placed,
        out_specs=(P(), P(), P("member", None), P("member"), P(), P(), P()), check_vma=False,
    )
```

```python
import functools

import jax
import jax.numpy as jnp
from jax import lax
from jax.experimental import pallas as pl
from jax.experimental.pallas import tpu as pltpu
from jax.sharding import PartitionSpec as P

learn_rate = 0.1
f32, bf16 = jnp.float32, jnp.bfloat16
TILE = 512
STEP = 256
STRIP = 16
BUNDLE = 32
LANES = 128
VMEM = pl.BlockSpec(memory_space=pltpu.VMEM)
HBM = pl.BlockSpec(memory_space=pltpu.HBM)
SMEM = pl.BlockSpec(memory_space=pltpu.SMEM)
shape = jax.ShapeDtypeStruct


def dot(lhs, rhs, contract=((1,), (0,))):
    return lax.dot_general(lhs, rhs, (contract, ((), ())), preferred_element_type=f32)


def pick_rows(column, first, count):
    ids = lax.broadcasted_iota(jnp.int32, (column.shape[0], count), 1) + first
    return jnp.where(column == ids, 1.0, 0.0).astype(bf16)


def spread_rows(row, ids):
    return jnp.where(row == ids, 1.0, 0.0).astype(bf16)


def row_ids(first, count, width):
    return lax.broadcasted_iota(jnp.int32, (count, width), 0) + first


def at(i, size):
    return pl.ds(pl.multiple_of(i * size, size), size)


def diagonal(count):
    ids = [lax.broadcasted_iota(jnp.int32, (count, count), k) for k in (0, 1)]
    return ids[0] == ids[1]


def to_column(row):
    return jnp.sum(jnp.where(diagonal(row.shape[1]), row, 0.0), 1, keepdims=True)


def to_row(column):
    return jnp.sum(jnp.where(diagonal(column.shape[0]), column, 0.0), 0, keepdims=True)


def requests_kernel(wanted_ref, out_ref):
    members, _, slots = out_ref.shape
    for member in range(members):
        out_ref[member] = wanted_ref[:, member * slots : (member + 1) * slots]


def serve_kernel(received_ref, half_ref, out_ref, hits, rows_out, sems):
    members, _, slots = received_ref.shape
    owned = half_ref.shape[0]
    ids = lax.broadcasted_iota(jnp.int32, (slots, owned), 1).astype(f32)
    copies = []
    for first in range(0, members * slots, TILE):
        for member in range(first // slots, (first + TILE) // slots):
            column = to_column(received_ref[member].astype(f32))
            hits[member * slots : (member + 1) * slots, :] = jnp.where(column == ids, 1.0, 0.0).astype(bf16)
        rows = pl.ds(first, TILE)
        rows_out[rows, :] = dot(hits[rows, :], half_ref[...]).astype(bf16)
        copies.append(pltpu.make_async_copy(rows_out.at[rows], out_ref.at[rows], sems.at[first // TILE]))
        copies[-1].start()
    for copy in copies:
        copy.wait()


def early_kernel(hot_ref, relation_ref, columns_ref, negative_column_ref, heads_ref, tails_ref, negatives_ref, relations_ref):
    hot, kinds = hot_ref.shape[0], relation_ref.shape[0]

    @pl.loop(0, negatives_ref.shape[0] // TILE)
    def _(i):
        rows = at(i, TILE)
        negatives_ref[rows, :] = dot(pick_rows(negative_column_ref[rows, :], 0, hot), hot_ref[...]).astype(bf16)

    @pl.loop(0, heads_ref.shape[0] // TILE)
    def _(i):
        rows = at(i, TILE)
        heads_ref[rows, :] = dot(pick_rows(columns_ref[rows, 0:1], 0, hot), hot_ref[...]).astype(bf16)
        tails_ref[rows, :] = dot(pick_rows(columns_ref[rows, 1:2], 0, hot), hot_ref[...]).astype(bf16)
        relations_ref[rows, :] = dot(pick_rows(columns_ref[rows, 2:3], 0, kinds), relation_ref[...]).astype(bf16)


def block_kernel(
    cold_hbm, heads_hbm, tails_hbm, negatives_hbm, relations_hbm, columns_hbm, negative_column_hbm, slots_ref,
    slot_grad_hbm, grads_hbm, relation_grads_hbm, loss_ref,
    cold_ref, heads, tails, negatives, relations, columns_ref, negative_column_ref,
    grads_ref, relation_grads_ref, slot_grad_ref, queries, score_grads, pos_grads, query_grads, sems_in, sems_out,
):
    batch, width = heads.shape
    neg, asked, half = negatives.shape[0], cold_ref.shape[0], width // 2
    hot = 768
    pairs = (
        (cold_hbm, cold_ref), (negative_column_hbm, negative_column_ref), (negatives_hbm, negatives),
        (columns_hbm, columns_ref), (heads_hbm, heads), (tails_hbm, tails), (relations_hbm, relations),
    )
    copies = [pltpu.make_async_copy(source, target, sems_in.at[k]) for k, (source, target) in enumerate(pairs)]
    for copy in copies[:3]:
        copy.start()
    for copy in copies[:3]:
        copy.wait()
    for copy in copies[3:]:
        copy.start()

    def add_cold(target, column_ref, lane):
        for i in range(target.shape[0] // STEP):
            rows = pl.ds(i * STEP, STEP)
            found = dot(pick_rows(column_ref[rows, lane : lane + 1], hot, asked), cold_ref[...])
            target[rows, :] = (found + target[rows, :].astype(f32)).astype(bf16)

    add_cold(negatives, negative_column_ref, 0)
    copies[3].wait()
    copies[4].wait()
    add_cold(heads, columns_ref, 0)
    copies[5].wait()
    add_cold(tails, columns_ref, 1)
    copies[6].wait()

    def parts(ref, rows):
        both = ref[rows, :].astype(f32)
        return both[:, :half], both[:, half:]

    @pl.loop(0, batch // STRIP, unroll=16)
    def _(i):
        rows = at(i, STRIP)
        head_real, head_imag = parts(heads, rows)
        relation_real, relation_imag = parts(relations, rows)
        query_real = head_real * relation_real - head_imag * relation_imag
        query_imag = head_real * relation_imag + head_imag * relation_real
        tail_real, tail_imag = parts(tails, rows)
        queries[rows, :half] = query_real.astype(bf16)
        queries[rows, half:] = query_imag.astype(bf16)
        pos_grads[rows, :] = jnp.sum(query_real * tail_real + query_imag * tail_imag, -1, keepdims=True)

    chunks = [pl.ds(k * LANES, LANES) for k in range(batch // LANES)]
    positive = jnp.concatenate([to_row(pos_grads[chunk, :]) for chunk in chunks])
    shrunk = jnp.exp(-jnp.abs(positive))
    loss_ref[...] = jnp.full_like(loss_ref, jnp.sum(jnp.maximum(-positive, 0.0) + jnp.log1p(shrunk)))
    pos_packed = jnp.where(positive >= 0, 1.0, shrunk) / (1.0 + shrunk) - 1.0
    for k, chunk in enumerate(chunks):
        pos_grads[chunk, :] = to_column(pos_packed[k : k + 1, :])

    for i in range(batch // STEP):
        rows = pl.ds(i * STEP, STEP)
        scores = dot(queries[rows, :], negatives[...], ((1,), (1,)))
        shrunk = jnp.exp(-jnp.abs(scores))
        loss = jnp.sum(jnp.maximum(scores, 0.0) + jnp.log1p(shrunk))
        sigmoid = jnp.where(scores >= 0, 1.0, shrunk) / (1.0 + shrunk)
        score_grads[rows, :] = (sigmoid / neg).astype(bf16)
        loss_ref[...] += loss / neg

    for i in range(batch // STEP):
        rows = pl.ds(i * STEP, STEP)
        query_grads[rows, :] = dot(score_grads[rows, :], negatives[...])

    grads_ref[2 * batch :, :] = dot(score_grads[...], queries[...], ((0,), (0,))).astype(bf16)

    @pl.loop(0, batch // STRIP, unroll=16)
    def _(i):
        rows = at(i, STRIP)
        head_real, head_imag = parts(heads, rows)
        relation_real, relation_imag = parts(relations, rows)
        tail_real, tail_imag = parts(tails, rows)
        pos = pos_grads[rows, :]
        grad_real = query_grads[rows, :half] + pos * tail_real
        grad_imag = query_grads[rows, half:] + pos * tail_imag
        grads_ref[rows, :half] = (grad_real * relation_real + grad_imag * relation_imag).astype(bf16)
        grads_ref[rows, half:] = (grad_imag * relation_real - grad_real * relation_imag).astype(bf16)
        relation_grads_ref[rows, :half] = (grad_real * head_real + grad_imag * head_imag).astype(bf16)
        relation_grads_ref[rows, half:] = (grad_imag * head_real - grad_real * head_imag).astype(bf16)
        later = pl.ds(pl.multiple_of(batch + i * STRIP, STRIP), STRIP)
        grads_ref[later, :half] = (pos * (head_real * relation_real - head_imag * relation_imag)).astype(bf16)
        grads_ref[later, half:] = (pos * (head_real * relation_imag + head_imag * relation_real)).astype(bf16)

    copies = [
        pltpu.make_async_copy(grads_ref, grads_hbm, sems_out.at[0]),
        pltpu.make_async_copy(relation_grads_ref, relation_grads_hbm, sems_out.at[1]),
    ]
    for copy in copies:
        copy.start()
    for i in range(asked // TILE):
        rows = pl.ds(i * TILE, TILE)
        hits = spread_rows(slots_ref[...], row_ids(hot + i * TILE, TILE, 1))
        slot_grad_ref[rows, :] = dot(hits, grads_ref[...]).astype(bf16)
        copies.append(pltpu.make_async_copy(slot_grad_ref.at[rows], slot_grad_hbm.at[rows], sems_out.at[2 + i]))
        copies[-1].start()
    for copy in copies:
        copy.wait()


def loss_pieces(loss, width):
    high = loss.astype(bf16).astype(f32)
    mid = (loss - high).astype(bf16).astype(f32)
    lane = lax.broadcasted_iota(jnp.int32, (1, width), 1)
    return jnp.where(lane == 0, high, jnp.where(lane == 1, mid, jnp.where(lane == 2, loss - high - mid, 0.0)))


def shared_kernel(loss_at, grads_ref, relation_grads_ref, places_ref, relation_places_ref, loss_ref, mine_ref, other_ref):
    count, width = mine_ref.shape
    pieces = loss_pieces(loss_ref[:1, :1], width)
    place = row_ids(0, count, 1)
    for i, out_ref in enumerate((mine_ref, other_ref)):
        ids = row_ids(i * count, count, 1)
        total = dot(spread_rows(places_ref[...], ids), grads_ref[...])
        total += dot(spread_rows(relation_places_ref[...], ids), relation_grads_ref[...])
        out_ref[...] = jnp.where(place % BUNDLE == loss_at, pieces, total).astype(out_ref.dtype)


def total_of(parts):
    return sum((part.astype(f32) for part in parts[1:]), parts[0].astype(f32))


def chip_sum_kernel(mine_ref, other_ref, shared_ref):
    shared_ref[...] = (mine_ref[...] + other_ref[...].astype(f32)).astype(bf16)


def group_rows(group, offsets, groups, piece):
    return jnp.concatenate([row_ids(lax.rem(group + offset, groups) * piece, piece, 1) for offset in offsets])


def owner_kernel(group_ref, row_ref, arrived_ref, _shared, _same, up_ref, down_ref, far_up_ref, far_down_ref, kept_ref):
    piece = far_up_ref.shape[0]
    ids = group_rows(group_ref[0], (1, 5, 7, 3, 2, 6, 0, 4), 8, piece)
    found = dot(spread_rows(row_ref[...], ids), arrived_ref[...])
    first = 0
    for ref in (up_ref, down_ref, far_up_ref, far_down_ref, kept_ref):
        ref[...] = found[first : first + ref.shape[0], :].astype(ref.dtype)
        first += ref.shape[0]


def near_sum_kernel(kept_ref, up_ref, down_ref, far_up_ref, far_down_ref, out_ref):
    piece = far_up_ref.shape[0]
    total = total_of([kept_ref[...], up_ref[...], down_ref[...]])
    out_ref[:piece, :] = total_of([total[:piece, :], far_up_ref[...], far_down_ref[...]]).astype(bf16)
    out_ref[piece:, :] = total[piece:, :].astype(bf16)


def with_loss(total, loss_at):
    loss = jnp.sum(total[loss_at : loss_at + 1, :], -1, keepdims=True)
    return jnp.where(row_ids(0, BUNDLE, 1) == loss_at, loss_pieces(loss, total.shape[1]), total).astype(bf16)


def member_sum_kernel(loss_at, parts_ref, _after, out_ref):
    out_ref[...] = with_loss(total_of([parts_ref[k] for k in range(parts_ref.shape[0])]), loss_at)


def pair_sum_kernel(loss_at, here_ref, there_ref, out_ref):
    out_ref[...] = with_loss(total_of([here_ref[...], there_ref[...]]), loss_at)


def group_sum_kernel(
    loss_at, batch_total, here_ref, there_ref, near_ref, across_ref, shared_ref, loss_ref, pair_ref, own_ref
):
    piece = own_ref.shape[0]
    own = total_of([near_ref[:piece, :], across_ref[piece:, :]]).astype(bf16)
    own_ref[...] = own
    pair_ref[:piece, :] = own
    pair_ref[piece:, :] = total_of([near_ref[piece:, :], across_ref[:piece, :]]).astype(bf16)
    total = total_of([here_ref[...], there_ref[...]])
    loss = jnp.sum(total[loss_at : loss_at + 1, :], -1, keepdims=True)
    loss_ref[...] = jnp.broadcast_to(loss / batch_total, loss_ref.shape)
    total = total.astype(bf16)
    for k in range(shared_ref.shape[0]):
        shared_ref[k] = total


def stepped(table, state_row, grad):
    new_state = to_column(state_row) + jnp.mean(grad * grad, -1, keepdims=True)
    return table - grad * (learn_rate / jnp.sqrt(new_state)), to_row(new_state)


def stream_steps(jobs, sems_in, sems_out):
    blocks = [(job, k) for job in jobs for k in range(job[1].shape[0] // LANES)]
    part = lambda k: pl.ds(k * LANES, LANES)
    loads = [
        pltpu.make_async_copy(job[0].at[part(k)], job[1].at[part(k)], sems_in.at[n]) for n, (job, k) in enumerate(blocks)
    ]
    stores = [
        pltpu.make_async_copy(job[5].at[part(k)], job[4].at[part(k)], sems_out.at[n]) for n, (job, k) in enumerate(blocks)
    ]
    for load in loads:
        load.start()

    def run():
        for load, store, (job, k) in zip(loads, stores, blocks):
            _, table, state, grad, _, result, new_state = job
            load.wait()
            result[part(k), :], new_state[k : k + 1, :] = stepped(
                table[part(k), :], state[k : k + 1, :], grad[part(k), :].astype(f32)
            )
            store.start()
        for store in stores:
            store.wait()

    return run


def cold_step_kernel(group_ref, table_hbm, state_ref, *refs):
    pieces, (new_table, new_state, table, result, grads, sems_in, sems_out) = refs[:-7], refs[-7:]
    run = stream_steps([(table_hbm, table, state_ref, grads, new_table, result, new_state)], sems_in, sems_out)
    for piece_ref, offsets in zip(pieces, ((0, 4), (7, 3), (1, 5), (6,), (2,))):
        size = piece_ref.shape[0] // len(offsets)
        for k, offset in enumerate(offsets):
            rows = at(lax.rem(group_ref[0] + offset, grads.shape[0] // size), size)
            grads[rows, :] = piece_ref[k * size : (k + 1) * size, :]
    run()


def shared_step_kernel(
    core_ref, mine_ref, other_ref, hot_hbm, hot_state, relation_hbm, relation_state, new_hot, new_hot_state, new_relation, new_relation_state,
    hot_table, hot_result, hot_grads, relation_table, relation_result, relation_grads, sems_in, sems_out,
):
    run = stream_steps(
        [
            (hot_hbm, hot_table, hot_state, hot_grads, new_hot, hot_result, new_hot_state),
            (relation_hbm, relation_table, relation_state, relation_grads, new_relation, relation_result, new_relation_state),
        ],
        sems_in, sems_out,
    )
    members = 2 * mine_ref.shape[0] // BUNDLE
    hot_part, relation_part = hot_grads.shape[0] // members, relation_grads.shape[0] // members
    first = core_ref[0] == 0
    for member in range(0, members, 2):
        rows = slice(member // 2 * BUNDLE, (member // 2 + 1) * BUNDLE)
        mine, other = mine_ref[rows, :].astype(f32), other_ref[rows, :].astype(f32)
        pair = (jnp.where(first, mine, other), jnp.where(first, other, mine))
        for k, grad in enumerate(pair):
            hot_grads[(member + k) * hot_part : (member + k + 1) * hot_part, :] = grad[:hot_part, :]
        relation_grads[member * relation_part : (member + 2) * relation_part, :] = jnp.concatenate(
            [grad[hot_part : hot_part + relation_part, :] for grad in pair]
        )
    run()


def call(kernel, name, out_shape, args, mib, flops=0, in_spaces=None, out_spaces=None, scratch=(), aliases=None):
    several = isinstance(out_shape, list)
    out_spaces = out_spaces or [VMEM] * (len(out_shape) if several else 1)
    return pl.pallas_call(
        kernel,
        out_shape=out_shape,
        in_specs=in_spaces or [VMEM] * len(args),
        out_specs=out_spaces if several else out_spaces[0],
        scratch_shapes=scratch,
        input_output_aliases=aliases or {},
        compiler_params=pltpu.CompilerParams(vmem_limit_bytes=mib * 2**20),
        cost_estimate=pl.CostEstimate(flops=flops, bytes_accessed=0, transcendentals=0),
        name=name,
    )(*args)


def exchange(array, axis, within=None):
    return lax.all_to_all(array, axis, split_axis=0, concat_axis=0, tiled=True, axis_index_groups=within)


def per_device(
    hot_table, hot_state, cold_table, cold_state, relation_table, relation_state,
    cold_requests, head_slots, relation_index, tail_slots, negative_slots,
):
    members, groups = lax.axis_size("member"), lax.axis_size("group")
    chips = members // 2
    width = hot_table.shape[1]
    hot, owned, relation_count = hot_table.shape[0], cold_table.shape[0], relation_table.shape[0]
    batch, neg = head_slots.shape[0], negative_slots.shape[1]
    asked = cold_requests.shape[1]
    hot_part, relation_part = hot // members, relation_count // members
    core = lax.axis_index("member") % 2
    group_at, core_at = lax.axis_index("group").reshape(1), core.reshape(1)
    same_core = [list(range(k, members, 2)) for k in (0, 1)]
    swap = [(m, m ^ 1) for m in range(members)]

    def place_of(owner, within):
        return ((owner % 2 ^ core) * chips + owner // 2) * BUNDLE + within

    wanted = call(requests_kernel, "requests", shape((members, 1, asked // members), jnp.int32), (cold_requests,), 61)
    received = exchange(wanted, "member")
    cold_half = cold_table.astype(bf16)
    served = call(
        serve_kernel, "serve", shape((asked, width), bf16), (received, cold_half), 61, 2 * asked * owned * width,
        out_spaces=[HBM],
        scratch=[
            pltpu.VMEM((asked, owned), bf16), pltpu.VMEM((asked, width), bf16),
            pltpu.SemaphoreType.DMA((asked // TILE,)),
        ],
    )
    returned = exchange(served.reshape(members, -1, width), "member").reshape(-1, width)

    columns = jnp.stack([head_slots, tail_slots, relation_index, relation_index]).T
    negative_column = negative_slots.reshape(-1, 1)
    slots = jnp.concatenate([head_slots, tail_slots, negative_slots.reshape(-1)])
    places = jnp.where(slots < hot, place_of(slots // hot_part, slots % hot_part), -1).reshape(1, -1)
    slots = slots.reshape(1, -1)
    relation_places = place_of(relation_index // relation_part, hot_part + relation_index % relation_part)

    rows, batch_rows = 2 * batch + neg, shape((batch, width), bf16)
    hot_heads, hot_tails, hot_negatives, relations = call(
        early_kernel, "early", [batch_rows, batch_rows, shape((neg, width), bf16), batch_rows],
        (hot_table.astype(bf16), relation_table.astype(bf16), columns, negative_column), 24,
        2 * rows * hot * width,
    )
    slot_grads, grads, relation_grads, loss = call(
        block_kernel, "block",
        [shape((asked, width), bf16), shape((rows, width), bf16), batch_rows, shape((8, 128), f32)],
        (returned, hot_heads, hot_tails, hot_negatives, relations, columns, negative_column, slots), 61,
        4 * rows * asked * width + 6 * batch * neg * width,
        in_spaces=[HBM] * 7 + [VMEM], out_spaces=[HBM] * 3 + [VMEM],
        scratch=[
            pltpu.VMEM((asked, width), bf16), pltpu.VMEM((batch, width), bf16), pltpu.VMEM((batch, width), bf16),
            pltpu.VMEM((neg, width), bf16), pltpu.VMEM((batch, width), bf16), pltpu.VMEM(columns.shape, jnp.int32),
            pltpu.VMEM((neg, 1), jnp.int32), pltpu.VMEM((rows, width), bf16), pltpu.VMEM((batch, width), bf16),
            pltpu.VMEM((asked, width), bf16), pltpu.VMEM((batch, width), bf16), pltpu.VMEM((batch, neg), bf16),
            pltpu.VMEM((batch, 1), f32), pltpu.VMEM((batch, width), f32), pltpu.SemaphoreType.DMA((7,)),
            pltpu.SemaphoreType.DMA((2 + asked // TILE,)),
        ],
    )
    arrived = exchange(slot_grads.reshape(members, -1, width), "member").reshape(-1, width)

    half, loss_at = chips * BUNDLE, hot_part + relation_part
    mine, other = call(
        functools.partial(shared_kernel, loss_at), "shared",
        [shape((half, width), f32), shape((half, width), bf16)],
        (grads, relation_grads, places, relation_places.reshape(1, -1), loss), 32, 4 * half * (rows + batch) * width,
    )
    other = lax.ppermute(other, "member", swap)
    shared = call(chip_sum_kernel, "chip_sum", shape((half, width), bf16), (mine, other), 8)
    piece = owned // groups
    one, two = shape((piece, width), bf16), shape((2 * piece, width), bf16)
    shared, up, down, far_up, far_down, kept = call(
        owner_kernel, "owner", [shape((half, width), bf16), two, two, one, one, shape((2 * piece, width), f32)],
        (group_at, received.reshape(1, -1), arrived, shared), 24, 2 * asked * owned * width,
        in_spaces=[SMEM, VMEM, VMEM, HBM], out_spaces=[HBM] + [VMEM] * 5, aliases={3: 0},
    )
    hop = lambda array, k: lax.ppermute(array, "group", [(g, (g + k) % groups) for g in range(groups)])
    near = call(near_sum_kernel, "near_sum", two, (kept, hop(up, 1), hop(down, -1), hop(far_up, 2), hop(far_down, -2)), 8)

    shared = exchange(shared.reshape(chips, -1, width), "member", same_core)
    shared = call(
        functools.partial(member_sum_kernel, loss_at), "member_sum", shape((BUNDLE, width), bf16),
        (shared, near), 8, in_spaces=[VMEM, HBM],
    )
    across = hop(near, 4)
    facing = lambda array, k: lax.ppermute(array, "group", [(g, g ^ k) for g in range(groups)])
    for k in (1, 2):
        shared = call(
            functools.partial(pair_sum_kernel, loss_at), "pair_sum", shape((BUNDLE, width), bf16),
            (shared, facing(shared, k)), 8,
        )
    shared, mean_loss, pair, own = call(
        functools.partial(group_sum_kernel, loss_at, batch * groups * members), "group_sum",
        [shape((chips, BUNDLE, width), bf16), shape((8, 128), f32), two, one],
        (shared, facing(shared, 4), near, across), 8,
    )
    sent = [hop(pair, 1), hop(pair, -1), hop(own, 2), hop(own, -2)]
    pieces = [pair] + sent
    mine = exchange(shared, "member", same_core).reshape(-1, width)
    mine = call(
        lambda *refs: None, "after_sent", shape(mine.shape, bf16), (mine, *sent), 8,
        in_spaces=[HBM] * (1 + len(sent)), out_spaces=[HBM], aliases={0: 0},
    )
    other = lax.ppermute(mine, "member", swap)
    state = lambda array: array.reshape(-1, LANES)
    buffers = lambda count: [pltpu.VMEM((count, width), f32), pltpu.VMEM((count, width), f32)]
    sems = lambda count: [pltpu.SemaphoreType.DMA((count // LANES,))] * 2
    new_cold_table, new_cold_state = call(
        cold_step_kernel, "cold_step", [shape((owned, width), f32), shape((owned // LANES, LANES), f32)],
        (group_at, cold_table, state(cold_state), *pieces), 61,
        in_spaces=[SMEM, HBM] + [VMEM] * (1 + len(pieces)), out_spaces=[HBM, VMEM],
        scratch=buffers(owned) + [pltpu.VMEM((owned, width), bf16)] + sems(owned),
    )
    new_hot_table, new_hot_state, new_relation_table, new_relation_state = call(
        shared_step_kernel, "shared_step",
        [
            shape((hot, width), f32), shape((hot // LANES, LANES), f32),
            shape((relation_count, width), f32), shape((relation_count // LANES, LANES), f32),
        ],
        (core_at, mine, other, hot_table, state(hot_state), relation_table, state(relation_state)), 61,
        in_spaces=[SMEM, VMEM, VMEM, HBM, VMEM, HBM, VMEM], out_spaces=[HBM, VMEM, HBM, VMEM],
        scratch=buffers(hot) + [pltpu.VMEM((hot, width), f32)] + buffers(relation_count)
        + [pltpu.VMEM((relation_count, width), f32)] + sems(hot + relation_count),
    )
    return (
        new_hot_table, new_hot_state.reshape(-1), new_cold_table, new_cold_state.reshape(-1),
        new_relation_table, new_relation_state.reshape(-1), mean_loss[0, 0],
    )


def solution(mesh):
    placed = (
        P(), P(), P("member", None), P("member"), P(), P(), P(("group", "member"), None),
        P(("group", "member")), P(("group", "member")), P(("group", "member")), P(("group", "member"), None),
    )
    return jax.shard_map(
        per_device, mesh=mesh, in_specs=placed,
        out_specs=(P(), P(), P("member", None), P("member"), P(), P(), P()), check_vma=False,
    )
```

```python
import functools

import jax
import jax.numpy as jnp
from jax import lax
from jax.experimental import pallas as pl
from jax.experimental.pallas import tpu as pltpu
from jax.sharding import PartitionSpec as P

learn_rate = 0.1
f32, bf16 = jnp.float32, jnp.bfloat16
TILE = 512
STEP = 256
STRIP = 16
BUNDLE = 32
LANES = 128
VMEM = pl.BlockSpec(memory_space=pltpu.VMEM)
HBM = pl.BlockSpec(memory_space=pltpu.HBM)
SMEM = pl.BlockSpec(memory_space=pltpu.SMEM)
shape = jax.ShapeDtypeStruct


def dot(lhs, rhs, contract=((1,), (0,))):
    return lax.dot_general(lhs, rhs, (contract, ((), ())), preferred_element_type=f32)


def pick_rows(column, first, count):
    ids = lax.broadcasted_iota(jnp.int32, (column.shape[0], count), 1) + first
    return jnp.where(column == ids, 1.0, 0.0).astype(bf16)


def spread_rows(row, ids):
    return jnp.where(row == ids, 1.0, 0.0).astype(bf16)


def row_ids(first, count, width):
    return lax.broadcasted_iota(jnp.int32, (count, width), 0) + first


def at(i, size):
    return pl.ds(pl.multiple_of(i * size, size), size)


def diagonal(count):
    ids = [lax.broadcasted_iota(jnp.int32, (count, count), k) for k in (0, 1)]
    return ids[0] == ids[1]


def to_column(row):
    return jnp.sum(jnp.where(diagonal(row.shape[1]), row, 0.0), 1, keepdims=True)


def to_row(column):
    return jnp.sum(jnp.where(diagonal(column.shape[0]), column, 0.0), 0, keepdims=True)


def requests_kernel(wanted_ref, out_ref):
    members, _, slots = out_ref.shape
    for member in range(members):
        out_ref[member] = wanted_ref[:, member * slots : (member + 1) * slots]


def serve_kernel(received_ref, half_ref, out_ref, hits, rows_out, sems):
    members, _, slots = received_ref.shape
    owned = half_ref.shape[0]
    ids = lax.broadcasted_iota(jnp.int32, (slots, owned), 1).astype(f32)
    copies = []
    for first in range(0, members * slots, TILE):
        for member in range(first // slots, (first + TILE) // slots):
            column = to_column(received_ref[member].astype(f32))
            hits[member * slots : (member + 1) * slots, :] = jnp.where(column == ids, 1.0, 0.0).astype(bf16)
        rows = pl.ds(first, TILE)
        rows_out[rows, :] = dot(hits[rows, :], half_ref[...]).astype(bf16)
        copies.append(pltpu.make_async_copy(rows_out.at[rows], out_ref.at[rows], sems.at[first // TILE]))
        copies[-1].start()
    for copy in copies:
        copy.wait()


def early_kernel(hot_ref, relation_ref, columns_ref, negative_column_ref, heads_ref, tails_ref, negatives_ref, relations_ref):
    hot, kinds = hot_ref.shape[0], relation_ref.shape[0]

    @pl.loop(0, negatives_ref.shape[0] // TILE)
    def _(i):
        rows = at(i, TILE)
        negatives_ref[rows, :] = dot(pick_rows(negative_column_ref[rows, :], 0, hot), hot_ref[...]).astype(bf16)

    @pl.loop(0, heads_ref.shape[0] // TILE)
    def _(i):
        rows = at(i, TILE)
        heads_ref[rows, :] = dot(pick_rows(columns_ref[rows, 0:1], 0, hot), hot_ref[...]).astype(bf16)
        tails_ref[rows, :] = dot(pick_rows(columns_ref[rows, 1:2], 0, hot), hot_ref[...]).astype(bf16)
        relations_ref[rows, :] = dot(pick_rows(columns_ref[rows, 2:3], 0, kinds), relation_ref[...]).astype(bf16)


def block_kernel(
    cold_hbm, heads_hbm, tails_hbm, negatives_hbm, relations_hbm, columns_hbm, negative_column_hbm, slots_ref,
    slot_grad_hbm, grads_hbm, relation_grads_hbm, loss_ref,
    cold_ref, heads, tails, negatives, relations, columns_ref, negative_column_ref,
    grads_ref, relation_grads_ref, slot_grad_ref, queries, score_grads, pos_grads, query_grads, sems_in, sems_out,
):
    batch, width = heads.shape
    neg, asked, half = negatives.shape[0], cold_ref.shape[0], width // 2
    hot = 768
    pairs = (
        (cold_hbm, cold_ref), (negative_column_hbm, negative_column_ref), (negatives_hbm, negatives),
        (columns_hbm, columns_ref), (heads_hbm, heads), (tails_hbm, tails), (relations_hbm, relations),
    )
    copies = [pltpu.make_async_copy(source, target, sems_in.at[k]) for k, (source, target) in enumerate(pairs)]
    for copy in copies:
        copy.start()
    for copy in copies[:3]:
        copy.wait()

    def add_cold(target, column_ref, lane):
        for i in range(target.shape[0] // STEP):
            rows = pl.ds(i * STEP, STEP)
            found = dot(pick_rows(column_ref[rows, lane : lane + 1], hot, asked), cold_ref[...])
            target[rows, :] = (found + target[rows, :].astype(f32)).astype(bf16)

    add_cold(negatives, negative_column_ref, 0)
    for copy in copies[3:]:
        copy.wait()
    add_cold(heads, columns_ref, 0)
    add_cold(tails, columns_ref, 1)

    def parts(ref, rows):
        both = ref[rows, :].astype(f32)
        return both[:, :half], both[:, half:]

    @pl.loop(0, batch // STRIP, unroll=16)
    def _(i):
        rows = at(i, STRIP)
        head_real, head_imag = parts(heads, rows)
        relation_real, relation_imag = parts(relations, rows)
        query_real = head_real * relation_real - head_imag * relation_imag
        query_imag = head_real * relation_imag + head_imag * relation_real
        tail_real, tail_imag = parts(tails, rows)
        queries[rows, :half] = query_real.astype(bf16)
        queries[rows, half:] = query_imag.astype(bf16)
        pos_grads[rows, :] = jnp.sum(query_real * tail_real + query_imag * tail_imag, -1, keepdims=True)

    positive = pos_grads[...]
    shrunk = jnp.exp(-jnp.abs(positive))
    loss_ref[...] = jnp.full_like(loss_ref, jnp.sum(jnp.maximum(-positive, 0.0) + jnp.log1p(shrunk)))
    pos_grads[...] = jnp.where(positive >= 0, 1.0, shrunk) / (1.0 + shrunk) - 1.0

    for i in range(batch // STEP):
        rows = pl.ds(i * STEP, STEP)
        scores = dot(queries[rows, :], negatives[...], ((1,), (1,)))
        shrunk = jnp.exp(-jnp.abs(scores))
        loss = jnp.sum(jnp.maximum(scores, 0.0) + jnp.log1p(shrunk))
        sigmoid = jnp.where(scores >= 0, 1.0, shrunk) / (1.0 + shrunk)
        score_grads[rows, :] = (sigmoid / neg).astype(bf16)
        loss_ref[...] += loss / neg

    for i in range(batch // STEP):
        rows = pl.ds(i * STEP, STEP)
        query_grads[rows, :] = dot(score_grads[rows, :], negatives[...])

    grads_ref[2 * batch :, :] = dot(score_grads[...], queries[...], ((0,), (0,))).astype(bf16)

    @pl.loop(0, batch // STRIP, unroll=16)
    def _(i):
        rows = at(i, STRIP)
        head_real, head_imag = parts(heads, rows)
        relation_real, relation_imag = parts(relations, rows)
        tail_real, tail_imag = parts(tails, rows)
        pos = pos_grads[rows, :]
        grad_real = query_grads[rows, :half] + pos * tail_real
        grad_imag = query_grads[rows, half:] + pos * tail_imag
        grads_ref[rows, :half] = (grad_real * relation_real + grad_imag * relation_imag).astype(bf16)
        grads_ref[rows, half:] = (grad_imag * relation_real - grad_real * relation_imag).astype(bf16)
        relation_grads_ref[rows, :half] = (grad_real * head_real + grad_imag * head_imag).astype(bf16)
        relation_grads_ref[rows, half:] = (grad_imag * head_real - grad_real * head_imag).astype(bf16)
        later = pl.ds(pl.multiple_of(batch + i * STRIP, STRIP), STRIP)
        grads_ref[later, :half] = (pos * (head_real * relation_real - head_imag * relation_imag)).astype(bf16)
        grads_ref[later, half:] = (pos * (head_real * relation_imag + head_imag * relation_real)).astype(bf16)

    copies = [
        pltpu.make_async_copy(grads_ref, grads_hbm, sems_out.at[0]),
        pltpu.make_async_copy(relation_grads_ref, relation_grads_hbm, sems_out.at[1]),
    ]
    for copy in copies:
        copy.start()
    for i in range(asked // TILE):
        rows = pl.ds(i * TILE, TILE)
        hits = spread_rows(slots_ref[...], row_ids(hot + i * TILE, TILE, 1))
        slot_grad_ref[rows, :] = dot(hits, grads_ref[...]).astype(bf16)
        copies.append(pltpu.make_async_copy(slot_grad_ref.at[rows], slot_grad_hbm.at[rows], sems_out.at[2 + i]))
        copies[-1].start()
    for copy in copies:
        copy.wait()


def loss_pieces(loss, width):
    high = loss.astype(bf16).astype(f32)
    mid = (loss - high).astype(bf16).astype(f32)
    lane = lax.broadcasted_iota(jnp.int32, (1, width), 1)
    return jnp.where(lane == 0, high, jnp.where(lane == 1, mid, jnp.where(lane == 2, loss - high - mid, 0.0)))


def shared_kernel(loss_at, grads_ref, relation_grads_ref, places_ref, relation_places_ref, loss_ref, mine_ref, other_ref):
    count, width = mine_ref.shape
    pieces = loss_pieces(loss_ref[:1, :1], width)
    place = row_ids(0, count, 1)
    for i, out_ref in enumerate((mine_ref, other_ref)):
        ids = row_ids(i * count, count, 1)
        total = dot(spread_rows(places_ref[...], ids), grads_ref[...])
        total += dot(spread_rows(relation_places_ref[...], ids), relation_grads_ref[...])
        out_ref[...] = jnp.where(place % BUNDLE == loss_at, pieces, total).astype(out_ref.dtype)


def total_of(parts):
    return sum((part.astype(f32) for part in parts[1:]), parts[0].astype(f32))


def chip_sum_kernel(mine_ref, other_ref, shared_ref):
    shared_ref[...] = (mine_ref[...] + other_ref[...].astype(f32)).astype(bf16)


def group_rows(group, offsets, groups, piece):
    return jnp.concatenate([row_ids(lax.rem(group + offset, groups) * piece, piece, 1) for offset in offsets])


def owner_kernel(group_ref, row_ref, arrived_ref, _shared, _same, up_ref, down_ref, far_up_ref, far_down_ref, kept_ref):
    piece = far_up_ref.shape[0]
    ids = group_rows(group_ref[0], (1, 5, 7, 3, 2, 6, 0, 4), 8, piece)
    found = dot(spread_rows(row_ref[...], ids), arrived_ref[...])
    first = 0
    for ref in (up_ref, down_ref, far_up_ref, far_down_ref, kept_ref):
        ref[...] = found[first : first + ref.shape[0], :].astype(ref.dtype)
        first += ref.shape[0]


def near_sum_kernel(kept_ref, up_ref, down_ref, far_up_ref, far_down_ref, out_ref):
    piece = far_up_ref.shape[0]
    total = total_of([kept_ref[...], up_ref[...], down_ref[...]])
    out_ref[:piece, :] = total_of([total[:piece, :], far_up_ref[...], far_down_ref[...]]).astype(bf16)
    out_ref[piece:, :] = total[piece:, :].astype(bf16)


def with_loss(total, loss_at):
    loss = jnp.sum(total[loss_at : loss_at + 1, :], -1, keepdims=True)
    return jnp.where(row_ids(0, BUNDLE, 1) == loss_at, loss_pieces(loss, total.shape[1]), total).astype(bf16)


def member_sum_kernel(loss_at, parts_ref, _after, out_ref):
    out_ref[...] = with_loss(total_of([parts_ref[k] for k in range(parts_ref.shape[0])]), loss_at)


def pair_sum_kernel(loss_at, here_ref, there_ref, out_ref):
    out_ref[...] = with_loss(total_of([here_ref[...], there_ref[...]]), loss_at)


def group_sum_kernel(
    loss_at, batch_total, here_ref, there_ref, near_ref, across_ref, shared_ref, loss_ref, pair_ref, own_ref
):
    piece = own_ref.shape[0]
    own = total_of([near_ref[:piece, :], across_ref[piece:, :]]).astype(bf16)
    own_ref[...] = own
    pair_ref[:piece, :] = own
    pair_ref[piece:, :] = total_of([near_ref[piece:, :], across_ref[:piece, :]]).astype(bf16)
    total = total_of([here_ref[...], there_ref[...]])
    loss = jnp.sum(total[loss_at : loss_at + 1, :], -1, keepdims=True)
    loss_ref[...] = jnp.broadcast_to(loss / batch_total, loss_ref.shape)
    total = total.astype(bf16)
    for k in range(shared_ref.shape[0]):
        shared_ref[k] = total


def stepped(table, state_row, grad):
    new_state = to_column(state_row) + jnp.mean(grad * grad, -1, keepdims=True)
    return table - grad * (learn_rate / jnp.sqrt(new_state)), to_row(new_state)


def stream_steps(jobs, sems_in, sems_out):
    blocks = [(job, k) for job in jobs for k in range(job[1].shape[0] // LANES)]
    part = lambda k: pl.ds(k * LANES, LANES)
    loads = [
        pltpu.make_async_copy(job[0].at[part(k)], job[1].at[part(k)], sems_in.at[n]) for n, (job, k) in enumerate(blocks)
    ]
    stores = [
        pltpu.make_async_copy(job[5].at[part(k)], job[4].at[part(k)], sems_out.at[n]) for n, (job, k) in enumerate(blocks)
    ]
    for load in loads:
        load.start()

    def run():
        for load, store, (job, k) in zip(loads, stores, blocks):
            _, table, state, grad, _, result, new_state = job
            load.wait()
            result[part(k), :], new_state[k : k + 1, :] = stepped(
                table[part(k), :], state[k : k + 1, :], grad[part(k), :].astype(f32)
            )
            store.start()
        for store in stores:
            store.wait()

    return run


def cold_step_kernel(group_ref, table_hbm, state_ref, *refs):
    pieces, (new_table, new_state, table, result, grads, sems_in, sems_out) = refs[:-7], refs[-7:]
    run = stream_steps([(table_hbm, table, state_ref, grads, new_table, result, new_state)], sems_in, sems_out)
    for piece_ref, offsets in zip(pieces, ((0, 4), (7, 3), (1, 5), (6,), (2,))):
        size = piece_ref.shape[0] // len(offsets)
        for k, offset in enumerate(offsets):
            rows = at(lax.rem(group_ref[0] + offset, grads.shape[0] // size), size)
            grads[rows, :] = piece_ref[k * size : (k + 1) * size, :]
    run()


def shared_step_kernel(
    core_ref, mine_ref, other_ref, hot_hbm, hot_state, relation_hbm, relation_state, new_hot, new_hot_state, new_relation, new_relation_state,
    hot_table, hot_result, hot_grads, relation_table, relation_result, relation_grads, sems_in, sems_out,
):
    run = stream_steps(
        [
            (hot_hbm, hot_table, hot_state, hot_grads, new_hot, hot_result, new_hot_state),
            (relation_hbm, relation_table, relation_state, relation_grads, new_relation, relation_result, new_relation_state),
        ],
        sems_in, sems_out,
    )
    members = 2 * mine_ref.shape[0] // BUNDLE
    hot_part, relation_part = hot_grads.shape[0] // members, relation_grads.shape[0] // members
    first = core_ref[0] == 0
    for member in range(0, members, 2):
        rows = slice(member // 2 * BUNDLE, (member // 2 + 1) * BUNDLE)
        mine, other = mine_ref[rows, :].astype(f32), other_ref[rows, :].astype(f32)
        pair = (jnp.where(first, mine, other), jnp.where(first, other, mine))
        for k, grad in enumerate(pair):
            hot_grads[(member + k) * hot_part : (member + k + 1) * hot_part, :] = grad[:hot_part, :]
        relation_grads[member * relation_part : (member + 2) * relation_part, :] = jnp.concatenate(
            [grad[hot_part : hot_part + relation_part, :] for grad in pair]
        )
    run()


def call(kernel, name, out_shape, args, mib, flops=0, in_spaces=None, out_spaces=None, scratch=(), aliases=None):
    several = isinstance(out_shape, list)
    out_spaces = out_spaces or [VMEM] * (len(out_shape) if several else 1)
    return pl.pallas_call(
        kernel,
        out_shape=out_shape,
        in_specs=in_spaces or [VMEM] * len(args),
        out_specs=out_spaces if several else out_spaces[0],
        scratch_shapes=scratch,
        input_output_aliases=aliases or {},
        compiler_params=pltpu.CompilerParams(vmem_limit_bytes=mib * 2**20),
        cost_estimate=pl.CostEstimate(flops=flops, bytes_accessed=0, transcendentals=0),
        name=name,
    )(*args)


def exchange(array, axis, within=None):
    return lax.all_to_all(array, axis, split_axis=0, concat_axis=0, tiled=True, axis_index_groups=within)


def per_device(
    hot_table, hot_state, cold_table, cold_state, relation_table, relation_state,
    cold_requests, head_slots, relation_index, tail_slots, negative_slots,
):
    members, groups = lax.axis_size("member"), lax.axis_size("group")
    chips = members // 2
    width = hot_table.shape[1]
    hot, owned, relation_count = hot_table.shape[0], cold_table.shape[0], relation_table.shape[0]
    batch, neg = head_slots.shape[0], negative_slots.shape[1]
    asked = cold_requests.shape[1]
    hot_part, relation_part = hot // members, relation_count // members
    core = lax.axis_index("member") % 2
    group_at, core_at = lax.axis_index("group").reshape(1), core.reshape(1)
    same_core = [list(range(k, members, 2)) for k in (0, 1)]
    swap = [(m, m ^ 1) for m in range(members)]

    def place_of(owner, within):
        return ((owner % 2 ^ core) * chips + owner // 2) * BUNDLE + within

    wanted = call(requests_kernel, "requests", shape((members, 1, asked // members), jnp.int32), (cold_requests,), 61)
    received = exchange(wanted, "member")
    cold_half = cold_table.astype(bf16)
    served = call(
        serve_kernel, "serve", shape((asked, width), bf16), (received, cold_half), 61, 2 * asked * owned * width,
        out_spaces=[HBM],
        scratch=[
            pltpu.VMEM((asked, owned), bf16), pltpu.VMEM((asked, width), bf16),
            pltpu.SemaphoreType.DMA((asked // TILE,)),
        ],
    )
    returned = exchange(served.reshape(members, -1, width), "member").reshape(-1, width)

    columns = jnp.stack([head_slots, tail_slots, relation_index, relation_index]).T
    negative_column = negative_slots.reshape(-1, 1)
    slots = jnp.concatenate([head_slots, tail_slots, negative_slots.reshape(-1)])
    places = jnp.where(slots < hot, place_of(slots // hot_part, slots % hot_part), -1).reshape(1, -1)
    slots = slots.reshape(1, -1)
    relation_places = place_of(relation_index // relation_part, hot_part + relation_index % relation_part)

    rows, batch_rows = 2 * batch + neg, shape((batch, width), bf16)
    hot_heads, hot_tails, hot_negatives, relations = call(
        early_kernel, "early", [batch_rows, batch_rows, shape((neg, width), bf16), batch_rows],
        (hot_table.astype(bf16), relation_table.astype(bf16), columns, negative_column), 24,
        2 * rows * hot * width,
    )
    slot_grads, grads, relation_grads, loss = call(
        block_kernel, "block",
        [shape((asked, width), bf16), shape((rows, width), bf16), batch_rows, shape((8, 128), f32)],
        (returned, hot_heads, hot_tails, hot_negatives, relations, columns, negative_column, slots), 61,
        4 * rows * asked * width + 6 * batch * neg * width,
        in_spaces=[HBM] * 7 + [VMEM], out_spaces=[HBM] * 3 + [VMEM],
        scratch=[
            pltpu.VMEM((asked, width), bf16), pltpu.VMEM((batch, width), bf16), pltpu.VMEM((batch, width), bf16),
            pltpu.VMEM((neg, width), bf16), pltpu.VMEM((batch, width), bf16), pltpu.VMEM(columns.shape, jnp.int32),
            pltpu.VMEM((neg, 1), jnp.int32), pltpu.VMEM((rows, width), bf16), pltpu.VMEM((batch, width), bf16),
            pltpu.VMEM((asked, width), bf16), pltpu.VMEM((batch, width), bf16), pltpu.VMEM((batch, neg), bf16),
            pltpu.VMEM((batch, 1), f32), pltpu.VMEM((batch, width), f32), pltpu.SemaphoreType.DMA((7,)),
            pltpu.SemaphoreType.DMA((2 + asked // TILE,)),
        ],
    )
    arrived = exchange(slot_grads.reshape(members, -1, width), "member").reshape(-1, width)

    half, loss_at = chips * BUNDLE, hot_part + relation_part
    mine, other = call(
        functools.partial(shared_kernel, loss_at), "shared",
        [shape((half, width), f32), shape((half, width), bf16)],
        (grads, relation_grads, places, relation_places.reshape(1, -1), loss), 32, 4 * half * (rows + batch) * width,
    )
    other = lax.ppermute(other, "member", swap)
    shared = call(chip_sum_kernel, "chip_sum", shape((half, width), bf16), (mine, other), 8)
    piece = owned // groups
    one, two = shape((piece, width), bf16), shape((2 * piece, width), bf16)
    shared, up, down, far_up, far_down, kept = call(
        owner_kernel, "owner", [shape((half, width), bf16), two, two, one, one, shape((2 * piece, width), f32)],
        (group_at, received.reshape(1, -1), arrived, shared), 24, 2 * asked * owned * width,
        in_spaces=[SMEM, VMEM, VMEM, HBM], out_spaces=[HBM] + [VMEM] * 5, aliases={3: 0},
    )
    hop = lambda array, k: lax.ppermute(array, "group", [(g, (g + k) % groups) for g in range(groups)])
    near = call(near_sum_kernel, "near_sum", two, (kept, hop(up, 1), hop(down, -1), hop(far_up, 2), hop(far_down, -2)), 8)

    shared = exchange(shared.reshape(chips, -1, width), "member", same_core)
    shared = call(
        functools.partial(member_sum_kernel, loss_at), "member_sum", shape((BUNDLE, width), bf16),
        (shared, near), 8, in_spaces=[VMEM, HBM],
    )
    across = hop(near, 4)
    facing = lambda array, k: lax.ppermute(array, "group", [(g, g ^ k) for g in range(groups)])
    for k in (1, 2):
        shared = call(
            functools.partial(pair_sum_kernel, loss_at), "pair_sum", shape((BUNDLE, width), bf16),
            (shared, facing(shared, k)), 8,
        )
    shared, mean_loss, pair, own = call(
        functools.partial(group_sum_kernel, loss_at, batch * groups * members), "group_sum",
        [shape((chips, BUNDLE, width), bf16), shape((8, 128), f32), two, one],
        (shared, facing(shared, 4), near, across), 8,
    )
    sent = [hop(pair, 1), hop(pair, -1), hop(own, 2), hop(own, -2)]
    pieces = [pair] + sent
    mine = exchange(shared, "member", same_core).reshape(-1, width)
    mine = call(
        lambda *refs: None, "after_sent", shape(mine.shape, bf16), (mine, *sent), 8,
        in_spaces=[HBM] * (1 + len(sent)), out_spaces=[HBM], aliases={0: 0},
    )
    other = lax.ppermute(mine, "member", swap)
    state = lambda array: array.reshape(-1, LANES)
    buffers = lambda count: [pltpu.VMEM((count, width), f32), pltpu.VMEM((count, width), f32)]
    sems = lambda count: [pltpu.SemaphoreType.DMA((count // LANES,))] * 2
    new_cold_table, new_cold_state = call(
        cold_step_kernel, "cold_step", [shape((owned, width), f32), shape((owned // LANES, LANES), f32)],
        (group_at, cold_table, state(cold_state), *pieces), 61,
        in_spaces=[SMEM, HBM] + [VMEM] * (1 + len(pieces)), out_spaces=[HBM, VMEM],
        scratch=buffers(owned) + [pltpu.VMEM((owned, width), bf16)] + sems(owned),
    )
    new_hot_table, new_hot_state, new_relation_table, new_relation_state = call(
        shared_step_kernel, "shared_step",
        [
            shape((hot, width), f32), shape((hot // LANES, LANES), f32),
            shape((relation_count, width), f32), shape((relation_count // LANES, LANES), f32),
        ],
        (core_at, mine, other, hot_table, state(hot_state), relation_table, state(relation_state)), 61,
        in_spaces=[SMEM, VMEM, VMEM, HBM, VMEM, HBM, VMEM], out_spaces=[HBM, VMEM, HBM, VMEM],
        scratch=buffers(hot) + [pltpu.VMEM((hot, width), f32)] + buffers(relation_count)
        + [pltpu.VMEM((relation_count, width), f32)] + sems(hot + relation_count),
    )
    return (
        new_hot_table, new_hot_state.reshape(-1), new_cold_table, new_cold_state.reshape(-1),
        new_relation_table, new_relation_state.reshape(-1), mean_loss[0, 0],
    )


def solution(mesh):
    placed = (
        P(), P(), P("member", None), P("member"), P(), P(), P(("group", "member"), None),
        P(("group", "member")), P(("group", "member")), P(("group", "member")), P(("group", "member"), None),
    )
    return jax.shard_map(
        per_device, mesh=mesh, in_specs=placed,
        out_specs=(P(), P(), P("member", None), P("member"), P(), P(), P()), check_vma=False,
    )
```

```python
import functools

import jax
import jax.numpy as jnp
from jax import lax
from jax.experimental import pallas as pl
from jax.experimental.pallas import tpu as pltpu
from jax.sharding import PartitionSpec as P

learn_rate = 0.1
f32, bf16 = jnp.float32, jnp.bfloat16
TILE = 512
STEP = 256
STRIP = 16
BUNDLE = 32
LANES = 128
VMEM = pl.BlockSpec(memory_space=pltpu.VMEM)
HBM = pl.BlockSpec(memory_space=pltpu.HBM)
SMEM = pl.BlockSpec(memory_space=pltpu.SMEM)
shape = jax.ShapeDtypeStruct


def dot(lhs, rhs, contract=((1,), (0,))):
    return lax.dot_general(lhs, rhs, (contract, ((), ())), preferred_element_type=f32)


def pick_rows(column, first, count):
    ids = lax.broadcasted_iota(jnp.int32, (column.shape[0], count), 1) + first
    return jnp.where(column == ids, 1.0, 0.0).astype(bf16)


def spread_rows(row, ids):
    return jnp.where(row == ids, 1.0, 0.0).astype(bf16)


def row_ids(first, count, width):
    return lax.broadcasted_iota(jnp.int32, (count, width), 0) + first


def at(i, size):
    return pl.ds(pl.multiple_of(i * size, size), size)


def diagonal(count):
    ids = [lax.broadcasted_iota(jnp.int32, (count, count), k) for k in (0, 1)]
    return ids[0] == ids[1]


def to_column(row):
    return jnp.sum(jnp.where(diagonal(row.shape[1]), row, 0.0), 1, keepdims=True)


def to_row(column):
    return jnp.sum(jnp.where(diagonal(column.shape[0]), column, 0.0), 0, keepdims=True)


def requests_kernel(wanted_ref, out_ref):
    members, _, slots = out_ref.shape
    for member in range(members):
        out_ref[member] = wanted_ref[:, member * slots : (member + 1) * slots]


def serve_kernel(received_ref, half_ref, out_ref, hits, rows_out, sems):
    members, _, slots = received_ref.shape
    owned = half_ref.shape[0]
    ids = lax.broadcasted_iota(jnp.int32, (slots, owned), 1).astype(f32)
    copies = []
    for first in range(0, members * slots, TILE):
        for member in range(first // slots, (first + TILE) // slots):
            column = to_column(received_ref[member].astype(f32))
            hits[member * slots : (member + 1) * slots, :] = jnp.where(column == ids, 1.0, 0.0).astype(bf16)
        rows = pl.ds(first, TILE)
        rows_out[rows, :] = dot(hits[rows, :], half_ref[...]).astype(bf16)
        copies.append(pltpu.make_async_copy(rows_out.at[rows], out_ref.at[rows], sems.at[first // TILE]))
        copies[-1].start()
    for copy in copies:
        copy.wait()


def early_kernel(hot_ref, relation_ref, columns_ref, negative_column_ref, heads_ref, tails_ref, negatives_ref, relations_ref):
    hot, kinds = hot_ref.shape[0], relation_ref.shape[0]

    @pl.loop(0, negatives_ref.shape[0] // TILE)
    def _(i):
        rows = at(i, TILE)
        negatives_ref[rows, :] = dot(pick_rows(negative_column_ref[rows, :], 0, hot), hot_ref[...]).astype(bf16)

    @pl.loop(0, heads_ref.shape[0] // TILE)
    def _(i):
        rows = at(i, TILE)
        heads_ref[rows, :] = dot(pick_rows(columns_ref[rows, 0:1], 0, hot), hot_ref[...]).astype(bf16)
        tails_ref[rows, :] = dot(pick_rows(columns_ref[rows, 1:2], 0, hot), hot_ref[...]).astype(bf16)
        relations_ref[rows, :] = dot(pick_rows(columns_ref[rows, 2:3], 0, kinds), relation_ref[...]).astype(bf16)


def block_kernel(
    cold_hbm, heads_hbm, tails_hbm, negatives_hbm, relations_hbm, columns_hbm, negative_column_hbm, slots_ref,
    slot_grad_hbm, grads_hbm, relation_grads_hbm, loss_ref,
    cold_ref, heads, tails, negatives, relations, columns_ref, negative_column_ref,
    grads_ref, relation_grads_ref, slot_grad_ref, queries, score_grads, pos_grads, query_grads, sems_in, sems_out,
):
    batch, width = heads.shape
    neg, asked, half = negatives.shape[0], cold_ref.shape[0], width // 2
    hot = 768
    pairs = (
        (cold_hbm, cold_ref), (negative_column_hbm, negative_column_ref), (negatives_hbm, negatives),
        (columns_hbm, columns_ref), (heads_hbm, heads), (tails_hbm, tails), (relations_hbm, relations),
    )
    copies = [pltpu.make_async_copy(source, target, sems_in.at[k]) for k, (source, target) in enumerate(pairs)]
    for copy in copies:
        copy.start()
    for copy in copies[:3]:
        copy.wait()

    def add_cold(target, column_ref, lane):
        for i in range(target.shape[0] // STEP):
            rows = pl.ds(i * STEP, STEP)
            found = dot(pick_rows(column_ref[rows, lane : lane + 1], hot, asked), cold_ref[...])
            target[rows, :] = (found + target[rows, :].astype(f32)).astype(bf16)

    add_cold(negatives, negative_column_ref, 0)
    for copy in copies[3:]:
        copy.wait()
    add_cold(heads, columns_ref, 0)
    add_cold(tails, columns_ref, 1)

    def parts(ref, rows):
        both = ref[rows, :].astype(f32)
        return both[:, :half], both[:, half:]

    @pl.loop(0, batch // STRIP, unroll=16)
    def _(i):
        rows = at(i, STRIP)
        head_real, head_imag = parts(heads, rows)
        relation_real, relation_imag = parts(relations, rows)
        query_real = head_real * relation_real - head_imag * relation_imag
        query_imag = head_real * relation_imag + head_imag * relation_real
        tail_real, tail_imag = parts(tails, rows)
        queries[rows, :half] = query_real.astype(bf16)
        queries[rows, half:] = query_imag.astype(bf16)
        pos_grads[rows, :] = jnp.sum(query_real * tail_real + query_imag * tail_imag, -1, keepdims=True)

    positive = pos_grads[...]
    shrunk = jnp.exp(-jnp.abs(positive))
    loss_ref[...] = jnp.full_like(loss_ref, jnp.sum(jnp.maximum(-positive, 0.0) + jnp.log1p(shrunk)))
    pos_grads[...] = jnp.where(positive >= 0, 1.0, shrunk) / (1.0 + shrunk) - 1.0

    for i in range(batch // STEP):
        rows = pl.ds(i * STEP, STEP)
        scores = dot(queries[rows, :], negatives[...], ((1,), (1,)))
        shrunk = jnp.exp(-jnp.abs(scores))
        loss = jnp.sum(jnp.maximum(scores, 0.0) + jnp.log1p(shrunk))
        sigmoid = jnp.where(scores >= 0, 1.0, shrunk) / (1.0 + shrunk)
        score_grads[rows, :] = (sigmoid / neg).astype(bf16)
        loss_ref[...] += loss / neg

    for i in range(batch // STEP):
        rows = pl.ds(i * STEP, STEP)
        query_grads[rows, :] = dot(score_grads[rows, :], negatives[...])

    grads_ref[2 * batch :, :] = dot(score_grads[...], queries[...], ((0,), (0,))).astype(bf16)

    @pl.loop(0, batch // STRIP, unroll=16)
    def _(i):
        rows = at(i, STRIP)
        head_real, head_imag = parts(heads, rows)
        relation_real, relation_imag = parts(relations, rows)
        tail_real, tail_imag = parts(tails, rows)
        pos = pos_grads[rows, :]
        grad_real = query_grads[rows, :half] + pos * tail_real
        grad_imag = query_grads[rows, half:] + pos * tail_imag
        grads_ref[rows, :half] = (grad_real * relation_real + grad_imag * relation_imag).astype(bf16)
        grads_ref[rows, half:] = (grad_imag * relation_real - grad_real * relation_imag).astype(bf16)
        relation_grads_ref[rows, :half] = (grad_real * head_real + grad_imag * head_imag).astype(bf16)
        relation_grads_ref[rows, half:] = (grad_imag * head_real - grad_real * head_imag).astype(bf16)
        later = pl.ds(pl.multiple_of(batch + i * STRIP, STRIP), STRIP)
        grads_ref[later, :half] = (pos * (head_real * relation_real - head_imag * relation_imag)).astype(bf16)
        grads_ref[later, half:] = (pos * (head_real * relation_imag + head_imag * relation_real)).astype(bf16)

    copies = [
        pltpu.make_async_copy(grads_ref, grads_hbm, sems_out.at[0]),
        pltpu.make_async_copy(relation_grads_ref, relation_grads_hbm, sems_out.at[1]),
    ]
    for copy in copies:
        copy.start()
    for i in range(asked // TILE):
        rows = pl.ds(i * TILE, TILE)
        hits = spread_rows(slots_ref[...], row_ids(hot + i * TILE, TILE, 1))
        slot_grad_ref[rows, :] = dot(hits, grads_ref[...]).astype(bf16)
        copies.append(pltpu.make_async_copy(slot_grad_ref.at[rows], slot_grad_hbm.at[rows], sems_out.at[2 + i]))
        copies[-1].start()
    for copy in copies:
        copy.wait()


def loss_pieces(loss, width):
    high = loss.astype(bf16).astype(f32)
    mid = (loss - high).astype(bf16).astype(f32)
    lane = lax.broadcasted_iota(jnp.int32, (1, width), 1)
    return jnp.where(lane == 0, high, jnp.where(lane == 1, mid, jnp.where(lane == 2, loss - high - mid, 0.0)))


def shared_kernel(loss_at, grads_ref, relation_grads_ref, places_ref, relation_places_ref, loss_ref, mine_ref, other_ref):
    count, width = mine_ref.shape
    pieces = loss_pieces(loss_ref[:1, :1], width)
    place = row_ids(0, count, 1)
    for i, out_ref in enumerate((mine_ref, other_ref)):
        ids = row_ids(i * count, count, 1)
        total = dot(spread_rows(places_ref[...], ids), grads_ref[...])
        total += dot(spread_rows(relation_places_ref[...], ids), relation_grads_ref[...])
        out_ref[...] = jnp.where(place % BUNDLE == loss_at, pieces, total).astype(out_ref.dtype)


def total_of(parts):
    return sum((part.astype(f32) for part in parts[1:]), parts[0].astype(f32))


def chip_sum_kernel(mine_ref, other_ref, shared_ref):
    shared_ref[...] = (mine_ref[...] + other_ref[...].astype(f32)).astype(bf16)


def group_rows(group, offsets, groups, piece):
    return jnp.concatenate([row_ids(lax.rem(group + offset, groups) * piece, piece, 1) for offset in offsets])


def owner_kernel(group_ref, row_ref, arrived_ref, _shared, _same, up_ref, down_ref, far_up_ref, far_down_ref, kept_ref):
    piece = far_up_ref.shape[0]
    ids = group_rows(group_ref[0], (1, 5, 7, 3, 2, 6, 0, 4), 8, piece)
    found = dot(spread_rows(row_ref[...], ids), arrived_ref[...])
    first = 0
    for ref in (up_ref, down_ref, far_up_ref, far_down_ref, kept_ref):
        ref[...] = found[first : first + ref.shape[0], :].astype(ref.dtype)
        first += ref.shape[0]


def near_sum_kernel(kept_ref, up_ref, down_ref, far_up_ref, far_down_ref, out_ref):
    piece = far_up_ref.shape[0]
    total = total_of([kept_ref[...], up_ref[...], down_ref[...]])
    out_ref[:piece, :] = total_of([total[:piece, :], far_up_ref[...], far_down_ref[...]]).astype(bf16)
    out_ref[piece:, :] = total[piece:, :].astype(bf16)


def with_loss(total, loss_at):
    loss = jnp.sum(total[loss_at : loss_at + 1, :], -1, keepdims=True)
    return jnp.where(row_ids(0, BUNDLE, 1) == loss_at, loss_pieces(loss, total.shape[1]), total).astype(bf16)


def member_sum_kernel(loss_at, parts_ref, _after, out_ref):
    out_ref[...] = with_loss(total_of([parts_ref[k] for k in range(parts_ref.shape[0])]), loss_at)


def pair_sum_kernel(loss_at, here_ref, there_ref, out_ref):
    out_ref[...] = with_loss(total_of([here_ref[...], there_ref[...]]), loss_at)


def group_sum_kernel(
    loss_at, batch_total, here_ref, there_ref, near_ref, across_ref, shared_ref, loss_ref, pair_ref, own_ref
):
    piece = own_ref.shape[0]
    own = total_of([near_ref[:piece, :], across_ref[piece:, :]]).astype(bf16)
    own_ref[...] = own
    pair_ref[:piece, :] = own
    pair_ref[piece:, :] = total_of([near_ref[piece:, :], across_ref[:piece, :]]).astype(bf16)
    total = total_of([here_ref[...], there_ref[...]])
    loss = jnp.sum(total[loss_at : loss_at + 1, :], -1, keepdims=True)
    loss_ref[...] = jnp.broadcast_to(loss / batch_total, loss_ref.shape)
    total = total.astype(bf16)
    for k in range(shared_ref.shape[0]):
        shared_ref[k] = total


def stepped(table, state_row, grad):
    new_state = to_column(state_row) + jnp.mean(grad * grad, -1, keepdims=True)
    return table - grad * (learn_rate / jnp.sqrt(new_state)), to_row(new_state)


def stream_steps(jobs, sems_in, sems_out):
    blocks = [(job, k) for job in jobs for k in range(job[1].shape[0] // LANES)]
    part = lambda k: pl.ds(k * LANES, LANES)
    loads = [
        pltpu.make_async_copy(job[0].at[part(k)], job[1].at[part(k)], sems_in.at[n]) for n, (job, k) in enumerate(blocks)
    ]
    stores = [
        pltpu.make_async_copy(job[5].at[part(k)], job[4].at[part(k)], sems_out.at[n]) for n, (job, k) in enumerate(blocks)
    ]
    for load in loads:
        load.start()

    def run():
        for load, store, (job, k) in zip(loads, stores, blocks):
            _, table, state, grad, _, result, new_state = job
            load.wait()
            result[part(k), :], new_state[k : k + 1, :] = stepped(
                table[part(k), :], state[k : k + 1, :], grad[part(k), :].astype(f32)
            )
            store.start()
        for store in stores:
            store.wait()

    return run


def cold_step_kernel(group_ref, table_hbm, state_ref, *refs):
    pieces, (new_table, new_state, table, result, grads, sems_in, sems_out) = refs[:-7], refs[-7:]
    run = stream_steps([(table_hbm, table, state_ref, grads, new_table, result, new_state)], sems_in, sems_out)
    for piece_ref, offsets in zip(pieces, ((0, 4), (7, 3), (1, 5), (6,), (2,))):
        size = piece_ref.shape[0] // len(offsets)
        for k, offset in enumerate(offsets):
            rows = at(lax.rem(group_ref[0] + offset, grads.shape[0] // size), size)
            grads[rows, :] = piece_ref[k * size : (k + 1) * size, :]
    run()


def shared_step_kernel(
    core_ref, mine_ref, other_ref, hot_hbm, hot_state, relation_hbm, relation_state, new_hot, new_hot_state, new_relation, new_relation_state,
    hot_table, hot_result, hot_grads, relation_table, relation_result, relation_grads, sems_in, sems_out,
):
    run = stream_steps(
        [
            (hot_hbm, hot_table, hot_state, hot_grads, new_hot, hot_result, new_hot_state),
            (relation_hbm, relation_table, relation_state, relation_grads, new_relation, relation_result, new_relation_state),
        ],
        sems_in, sems_out,
    )
    members = 2 * mine_ref.shape[0] // BUNDLE
    hot_part, relation_part = hot_grads.shape[0] // members, relation_grads.shape[0] // members
    first = core_ref[0] == 0
    for member in range(0, members, 2):
        rows = slice(member // 2 * BUNDLE, (member // 2 + 1) * BUNDLE)
        mine, other = mine_ref[rows, :].astype(f32), other_ref[rows, :].astype(f32)
        pair = (jnp.where(first, mine, other), jnp.where(first, other, mine))
        for k, grad in enumerate(pair):
            hot_grads[(member + k) * hot_part : (member + k + 1) * hot_part, :] = grad[:hot_part, :]
        relation_grads[member * relation_part : (member + 2) * relation_part, :] = jnp.concatenate(
            [grad[hot_part : hot_part + relation_part, :] for grad in pair]
        )
    run()


def call(kernel, name, out_shape, args, mib, flops=0, in_spaces=None, out_spaces=None, scratch=(), aliases=None):
    several = isinstance(out_shape, list)
    out_spaces = out_spaces or [VMEM] * (len(out_shape) if several else 1)
    return pl.pallas_call(
        kernel,
        out_shape=out_shape,
        in_specs=in_spaces or [VMEM] * len(args),
        out_specs=out_spaces if several else out_spaces[0],
        scratch_shapes=scratch,
        input_output_aliases=aliases or {},
        compiler_params=pltpu.CompilerParams(vmem_limit_bytes=mib * 2**20),
        cost_estimate=pl.CostEstimate(flops=flops, bytes_accessed=0, transcendentals=0),
        name=name,
    )(*args)


def exchange(array, axis, within=None):
    return lax.all_to_all(array, axis, split_axis=0, concat_axis=0, tiled=True, axis_index_groups=within)


def per_device(
    hot_table, hot_state, cold_table, cold_state, relation_table, relation_state,
    cold_requests, head_slots, relation_index, tail_slots, negative_slots,
):
    members, groups = lax.axis_size("member"), lax.axis_size("group")
    chips = members // 2
    width = hot_table.shape[1]
    hot, owned, relation_count = hot_table.shape[0], cold_table.shape[0], relation_table.shape[0]
    batch, neg = head_slots.shape[0], negative_slots.shape[1]
    asked = cold_requests.shape[1]
    hot_part, relation_part = hot // members, relation_count // members
    core = lax.axis_index("member") % 2
    group_at, core_at = lax.axis_index("group").reshape(1), core.reshape(1)
    same_core = [list(range(k, members, 2)) for k in (0, 1)]
    swap = [(m, m ^ 1) for m in range(members)]

    def place_of(owner, within):
        return ((owner % 2 ^ core) * chips + owner // 2) * BUNDLE + within

    wanted = call(requests_kernel, "requests", shape((members, 1, asked // members), jnp.int32), (cold_requests,), 61)
    received = exchange(wanted, "member")
    cold_half = cold_table.astype(bf16)
    served = call(
        serve_kernel, "serve", shape((asked, width), bf16), (received, cold_half), 61, 2 * asked * owned * width,
        out_spaces=[HBM],
        scratch=[
            pltpu.VMEM((asked, owned), bf16), pltpu.VMEM((asked, width), bf16),
            pltpu.SemaphoreType.DMA((asked // TILE,)),
        ],
    )
    returned = exchange(served.reshape(members, -1, width), "member").reshape(-1, width)

    columns = jnp.stack([head_slots, tail_slots, relation_index, relation_index]).T
    negative_column = negative_slots.reshape(-1, 1)
    slots = jnp.concatenate([head_slots, tail_slots, negative_slots.reshape(-1)])
    places = jnp.where(slots < hot, place_of(slots // hot_part, slots % hot_part), -1).reshape(1, -1)
    slots = slots.reshape(1, -1)
    relation_places = place_of(relation_index // relation_part, hot_part + relation_index % relation_part)

    rows, batch_rows = 2 * batch + neg, shape((batch, width), bf16)
    hot_heads, hot_tails, hot_negatives, relations = call(
        early_kernel, "early", [batch_rows, batch_rows, shape((neg, width), bf16), batch_rows],
        (hot_table.astype(bf16), relation_table.astype(bf16), columns, negative_column), 24,
        2 * rows * hot * width,
    )
    slot_grads, grads, relation_grads, loss = call(
        block_kernel, "block",
        [shape((asked, width), bf16), shape((rows, width), bf16), batch_rows, shape((8, 128), f32)],
        (returned, hot_heads, hot_tails, hot_negatives, relations, columns, negative_column, slots), 61,
        4 * rows * asked * width + 6 * batch * neg * width,
        in_spaces=[HBM] * 7 + [VMEM], out_spaces=[HBM] * 3 + [VMEM],
        scratch=[
            pltpu.VMEM((asked, width), bf16), pltpu.VMEM((batch, width), bf16), pltpu.VMEM((batch, width), bf16),
            pltpu.VMEM((neg, width), bf16), pltpu.VMEM((batch, width), bf16), pltpu.VMEM(columns.shape, jnp.int32),
            pltpu.VMEM((neg, 1), jnp.int32), pltpu.VMEM((rows, width), bf16), pltpu.VMEM((batch, width), bf16),
            pltpu.VMEM((asked, width), bf16), pltpu.VMEM((batch, width), bf16), pltpu.VMEM((batch, neg), bf16),
            pltpu.VMEM((batch, 1), f32), pltpu.VMEM((batch, width), f32), pltpu.SemaphoreType.DMA((7,)),
            pltpu.SemaphoreType.DMA((2 + asked // TILE,)),
        ],
    )
    arrived = exchange(slot_grads.reshape(members, -1, width), "member").reshape(-1, width)

    half, loss_at = chips * BUNDLE, hot_part + relation_part
    mine, other = call(
        functools.partial(shared_kernel, loss_at), "shared",
        [shape((half, width), f32), shape((half, width), bf16)],
        (grads, relation_grads, places, relation_places.reshape(1, -1), loss), 32, 4 * half * (rows + batch) * width,
    )
    other = lax.ppermute(other, "member", swap)
    shared = call(chip_sum_kernel, "chip_sum", shape((half, width), bf16), (mine, other), 8)
    piece = owned // groups
    one, two = shape((piece, width), bf16), shape((2 * piece, width), bf16)
    shared, up, down, far_up, far_down, kept = call(
        owner_kernel, "owner", [shape((half, width), bf16), two, two, one, one, shape((2 * piece, width), f32)],
        (group_at, received.reshape(1, -1), arrived, shared), 24, 2 * asked * owned * width,
        in_spaces=[SMEM, VMEM, VMEM, HBM], out_spaces=[HBM] + [VMEM] * 5, aliases={3: 0},
    )
    hop = lambda array, k: lax.ppermute(array, "group", [(g, (g + k) % groups) for g in range(groups)])
    near = call(near_sum_kernel, "near_sum", two, (kept, hop(up, 1), hop(down, -1), hop(far_up, 2), hop(far_down, -2)), 8)

    shared = exchange(shared.reshape(chips, -1, width), "member", same_core)
    shared = call(
        functools.partial(member_sum_kernel, loss_at), "member_sum", shape((BUNDLE, width), bf16),
        (shared, near), 8, in_spaces=[VMEM, HBM],
    )
    across = hop(near, 4)
    facing = lambda array, k: lax.ppermute(array, "group", [(g, g ^ k) for g in range(groups)])
    for k in (1, 2):
        shared = call(
            functools.partial(pair_sum_kernel, loss_at), "pair_sum", shape((BUNDLE, width), bf16),
            (shared, facing(shared, k)), 8,
        )
    shared, mean_loss, pair, own = call(
        functools.partial(group_sum_kernel, loss_at, batch * groups * members), "group_sum",
        [shape((chips, BUNDLE, width), bf16), shape((8, 128), f32), two, one],
        (shared, facing(shared, 4), near, across), 8,
    )
    sent = [hop(pair, 1), hop(pair, -1), hop(own, 2), hop(own, -2)]
    pieces = [pair] + sent
    mine = exchange(shared, "member", same_core).reshape(-1, width)
    mine = call(
        lambda *refs: None, "after_sent", shape(mine.shape, bf16), (mine, *sent), 8,
        in_spaces=[HBM] * (1 + len(sent)), out_spaces=[HBM], aliases={0: 0},
    )
    other = lax.ppermute(mine, "member", swap)
    state = lambda array: array.reshape(-1, LANES)
    buffers = lambda count: [pltpu.VMEM((count, width), f32), pltpu.VMEM((count, width), f32)]
    sems = lambda count: [pltpu.SemaphoreType.DMA((count // LANES,))] * 2
    new_cold_table, new_cold_state = call(
        cold_step_kernel, "cold_step", [shape((owned, width), f32), shape((owned // LANES, LANES), f32)],
        (group_at, cold_table, state(cold_state), *pieces), 61,
        in_spaces=[SMEM, HBM] + [VMEM] * (1 + len(pieces)), out_spaces=[HBM, VMEM],
        scratch=buffers(owned) + [pltpu.VMEM((owned, width), bf16)] + sems(owned),
    )
    new_hot_table, new_hot_state, new_relation_table, new_relation_state = call(
        shared_step_kernel, "shared_step",
        [
            shape((hot, width), f32), shape((hot // LANES, LANES), f32),
            shape((relation_count, width), f32), shape((relation_count // LANES, LANES), f32),
        ],
        (core_at, mine, other, hot_table, state(hot_state), relation_table, state(relation_state)), 44,
        in_spaces=[SMEM, VMEM, VMEM, HBM, VMEM, HBM, VMEM], out_spaces=[HBM, VMEM, HBM, VMEM],
        scratch=buffers(hot) + [pltpu.VMEM((hot, width), f32)] + buffers(relation_count)
        + [pltpu.VMEM((relation_count, width), f32)] + sems(hot + relation_count),
    )
    return (
        new_hot_table, new_hot_state.reshape(-1), new_cold_table, new_cold_state.reshape(-1),
        new_relation_table, new_relation_state.reshape(-1), mean_loss[0, 0],
    )


def solution(mesh):
    placed = (
        P(), P(), P("member", None), P("member"), P(), P(), P(("group", "member"), None),
        P(("group", "member")), P(("group", "member")), P(("group", "member")), P(("group", "member"), None),
    )
    return jax.shard_map(
        per_device, mesh=mesh, in_specs=placed,
        out_specs=(P(), P(), P("member", None), P("member"), P(), P(), P()), check_vma=False,
    )
```
